32 devices in a mesh: dom: 8 (over z, x), rep: 4 (over y, core).
Axes of the slice: x: 2, y: 2, z: 4, core: 2. Of those that a mesh axis runs over, the one named last changes fastest.
Arguments:
- spline_blocks: bfloat16 [256, 2, 64, 128], P(('dom', 'rep')), may hold values from -0.75 to 0.75
- modal_coeff: bfloat16 [64, 2, 8], replicated, may hold values from -6 to 6
- frequency: float32 [8], replicated, may hold values from 0.2 to 0.8
- face_dest: int32 [32768, 1], P('dom'), may hold values from 0 to 7; in each aligned block of 4096 rows (0 to 4095, 4096 to 8191, ...) at most 1024 rows name the same one
- face_cell: int32 [32768], P('dom'), may hold values from 0 to 2047
- wall_weight: float32 [5, 2, 16384], P(None, None, 'dom'), may hold values from -6 to 6
- flow_rhs: float32 [5, 2, 8, 16384], P(None, None, 'rep', 'dom'), may hold values from -6 to 6
- previous: float32 [5, 2, 8, 16384], P(None, None, 'rep', 'dom'), may hold values from -6 to 6
- diag_inverse: float32 [5, 5, 16384], P(None, None, 'dom'), may hold values from -0.3 to 1.2
- off_jacobian: bfloat16 [6, 5, 5, 16384], P(None, None, None, 'dom'), may hold values from -0.5 to 0.5
- neighbor: int32 [6, 16384], P(None, 'dom'), may hold values from 0 to 3071, as said below
- send_list: int32 [4, 2048], P(None, 'dom'), may hold values from 0 to 2047
Outputs:
- solution: float32 [5, 2, 8, 16384], P(None, None, 'rep', 'dom')
The draws below stay inside these ranges and needn't reach their ends.
Inputs may be any that keep to these rules, and one draw needn't show every extreme that they name: `face_dest`: in each aligned block of 4096 rows (the rows of one index of dom), no partition is named by more than 1024 rows, and in every draw some partition is named by exactly 1024 rows of some block. `neighbor`: entries below 2048 name a cell of the same partition; entry 2048 + k * 256 + i names ghost row i of block k.
All inputs are finite; a program needn't handle non-finite values.
Results may differ from the reference program's by a relative error of at most 0.0003.
Values may be sent and summed in bfloat16 or wider, within the bound.
A program may use at most 64 MiB of HBM per device.

```python
import math
import jax
import jax.numpy as jnp
import numpy as np
from jax import lax

MODES = 64
PAIRS = 8
SWEEPS = 2
CELLS = 2048
HALO = 256
FACE_DOM = 4096
CAP = 1024
NFACES = 32768
NBLK = 256
NCELLS = 16384
NSEND = 2048
N_DOM = 8


def draw_diag_inverse(key, part):
    first_key, second_key = jax.random.split(jax.random.fold_in(key, 11))
    diagonal_part = jnp.minimum(jnp.exp(jax.random.uniform(first_key, (5, 5, NCELLS), jnp.float32, math.log(0.4), math.log(1.3))), 1.2)
    other_part = jnp.clip(0.15 * jax.random.normal(second_key, (5, 5, NCELLS), jnp.float32), -0.3, 0.3)
    identity = jnp.eye(5, dtype=jnp.float32)[:, :, None]
    return jnp.where(identity > 0.5, diagonal_part, other_part).astype(jnp.float32)


def draw_neighbor(key, part):
    pick_key, local_key, ghost_key = jax.random.split(jax.random.fold_in(key, 23), 3)
    chooser = jax.random.randint(pick_key, (6, NCELLS), 0, 8)
    local_rows = jax.random.randint(local_key, (6, NCELLS), 0, CELLS)
    ghost_rows = jax.random.randint(ghost_key, (6, NCELLS), CELLS, CELLS + 4 * HALO)
    return jnp.where(chooser == 0, ghost_rows, local_rows).astype(jnp.int32)


def with_ends(array, key, least, largest):
    shape = array.shape
    index_at = [jax.random.randint(jax.random.fold_in(key, axis), (), 0, shape[axis]) for axis in range(len(shape))]
    array = array.at[tuple(index_at)].set(least)
    longest = shape.index(max(shape))
    index_at[longest] = (index_at[longest] + 1) % shape[longest]
    return array.at[tuple(index_at)].set(largest)


def level_of(key, dims, shards, smallest, largest):
    gain = 1.0
    for axis_at, blocks in shards:
        steps = jax.random.uniform(jax.random.fold_in(jax.random.fold_in(key, 6), axis_at), (blocks,), jnp.float32, smallest / len(shards), largest / len(shards))
        gain = gain * jnp.repeat(jnp.exp(steps), dims[axis_at] // blocks).reshape((-1,) + (1,) * (len(dims) - 1 - axis_at))
    return gain


def assign_block(own_key, own, number, rows, amount, top, reach, slope):
    sequence = jax.random.permutation(own_key, amount)
    packed, ordinary = portions_of(amount, rows * top, reach, slope, True), portions_of(amount, rows * top, reach, slope, False)
    places = jnp.arange(amount)

    def named(lengths, turn):
        used = int((lengths > 0).sum())
        fixed = max(1, used // 4)
        shifted = fixed + (places - fixed + turn * (used - fixed)) % max(1, amount - fixed)
        return jnp.zeros((amount,), jnp.int32).at[sequence[jnp.where(places < fixed, places, shifted)]].set(jnp.asarray(lengths, jnp.int32))

    lengths = jnp.where(number % 4 == 0, named(packed, number // 4), named(ordinary, number - number // 4 - 1))
    mixed = jax.random.permutation(jax.random.fold_in(own, 3), amount)
    source_of, receiver = mixed[0:amount // 2 * 2:2], mixed[1:amount // 2 * 2:2]
    margin = jnp.minimum(lengths[source_of] - 1, reach - lengths[receiver]) // 2
    margin = jnp.where((source_of == sequence[0]) | (receiver == sequence[0]) | (lengths[receiver] == 0), 0, jnp.maximum(margin, 0))
    shifted = jax.random.randint(jax.random.fold_in(own, 4), (amount // 2,), 0, 1 << 20) % (margin + 1)
    lengths = lengths.at[source_of].add(-shifted).at[receiver].add(shifted)
    items = jnp.searchsorted(jnp.cumsum(lengths), jnp.arange(rows * top), side="right").astype(jnp.int32)
    listing = items.reshape(top, rows).T
    listing = listing[jax.random.permutation(jax.random.fold_in(own, 1), rows)]
    turn = jax.random.randint(jax.random.fold_in(own, 2), (rows, 1), 0, top)
    return jnp.take_along_axis(listing, (jnp.arange(top)[None, :] + turn) % top, axis=1)


def portions_of(amount, total, limit, lean, full):
    portions = [(1 << 20) // math.isqrt(rank ** lean) + 1 for rank in range(1, amount + 1)]
    largest = limit if full else min(limit, max(-(-total // amount), total * portions[0] // sum(portions)))
    least = 1 if total - largest >= amount - 1 else 0
    holding, spare = [largest] + [least] * (amount - 1), total - largest - least * (amount - 1)
    while spare > 0:
        movable = [i for i in range(1, amount) if holding[i] < largest] or [i for i in range(1, amount) if holding[i] < limit]
        mass, left = sum([portions[i] for i in movable]), spare
        for i in movable:
            more = min(limit - holding[i], max(1, left * portions[i] // mass), spare)
            holding[i] = holding[i] + more
            spare = spare - more
    return np.array(holding)


def noise(key, dims, width, bound, cuts=(), kind=jnp.bfloat16):
    factor_of = level_of(key, dims, cuts, -0.22, 0.18) if cuts else 1.0
    array = jax.random.normal(key, dims, jnp.float32) * width * factor_of
    return jnp.minimum(jnp.maximum(array, -bound), bound).astype(kind)


def setup_inputs(seed: int = 0) -> dict:
    streams_of = jax.random.split(jax.random.key(seed), 13)
    spline_blocks = noise(streams_of[0], (NBLK, 2, MODES, 128), MODES ** -0.5, 0.75, ((0, 32),))
    modal_coeff = noise(streams_of[1], (MODES, 2, PAIRS), 1.0, 6.0)
    frequency = jnp.clip(jnp.exp(jax.random.uniform(streams_of[2], (PAIRS,), jnp.float32, math.log(0.2), math.log(0.8))), 0.2, 0.8)
    face_dest_keys = jax.random.split(jax.random.fold_in(streams_of[3], 1), NFACES // FACE_DOM)
    face_dest_turns = jax.random.permutation(jax.random.fold_in(streams_of[3], 3), NFACES // FACE_DOM)
    face_dest = jax.vmap(lambda own, number: assign_block(jax.random.fold_in(streams_of[3], 2), own, number, FACE_DOM, N_DOM, 1, CAP, 2))(face_dest_keys, face_dest_turns).reshape((NFACES, 1))
    face_cell = with_ends(jax.random.randint(streams_of[4], (NFACES,), 0, CELLS), jax.random.fold_in(streams_of[4], 1), 0, CELLS - 1).astype(jnp.int32)
    wall_weight = noise(streams_of[5], (5, 2, NCELLS), 1.0, 6.0, ((2, 8),), jnp.float32)
    flow_rhs = noise(streams_of[6], (5, 2, PAIRS, NCELLS), 1.0, 6.0, ((2, 4), (3, 8)), jnp.float32)
    previous = noise(streams_of[7], (5, 2, PAIRS, NCELLS), 1.0, 6.0, ((2, 4), (3, 8)), jnp.float32)
    diag_inverse = draw_diag_inverse(jax.random.fold_in(streams_of[12], 71), 0)
    off_jacobian = noise(streams_of[9], (6, 5, 5, NCELLS), 0.08, 0.5, ((3, 8),))
    neighbor = draw_neighbor(jax.random.fold_in(streams_of[12], 71), 0)
    send_list = with_ends(jax.random.randint(streams_of[11], (4, NSEND), 0, CELLS), jax.random.fold_in(streams_of[11], 1), 0, CELLS - 1).astype(jnp.int32)
    return {"spline_blocks": spline_blocks, "modal_coeff": modal_coeff, "frequency": frequency, "face_dest": face_dest, "face_cell": face_cell, "wall_weight": wall_weight, "flow_rhs": flow_rhs, "previous": previous, "diag_inverse": diag_inverse, "off_jacobian": off_jacobian, "neighbor": neighbor, "send_list": send_list}


offsets = (1, -1, 2, -2)


def face_values(blocks_in, coeff_in, freq_in):
    mode_count = coeff_in.shape[0]
    column_count = coeff_in.shape[2]
    flat_coeff = coeff_in.astype(jnp.float32).reshape(mode_count, 2 * column_count)
    products = jnp.einsum("kqmr,mz->qzkr", blocks_in.astype(jnp.float32), flat_coeff, precision=lax.Precision.HIGHEST)
    products = products.reshape(2, 2, column_count, blocks_in.shape[0] * blocks_in.shape[3])
    angular = freq_in[:, None]
    velocity = jnp.stack([-angular * products[0, 1], angular * products[0, 0]])
    return jnp.stack([velocity, products[1]])


def reference(spline_blocks, modal_coeff, frequency, face_dest, face_cell, wall_weight, flow_rhs, previous, diag_inverse, off_jacobian, neighbor, send_list):
    face_data = face_values(spline_blocks, modal_coeff, frequency)
    target = (face_dest[:, 0] * CELLS + face_cell).astype(jnp.int32)
    wall_sum = jnp.zeros((2, 2, PAIRS, NCELLS), jnp.float32).at[:, :, :, target].add(face_data)
    rhs_full = flow_rhs + wall_weight[:, 0, None, None, :] * wall_sum[0][None] + wall_weight[:, 1, None, None, :] * wall_sum[1][None]
    send_rows = send_list.reshape(4, N_DOM, HALO)
    local_index = neighbor.reshape(6, N_DOM, CELLS)
    angular = frequency[None, :, None]
    iterate = previous
    for sweep_index in range(SWEEPS):
        parted = iterate.reshape(5, 2, PAIRS, N_DOM, CELLS)
        ghost_list = []
        for slot_index in range(4):
            picked = jnp.take_along_axis(parted, send_rows[slot_index][None, None, None], axis=4)
            ghost_list.append(jnp.roll(picked, offsets[slot_index], axis=3))
        extended = jnp.concatenate([parted] + ghost_list, axis=4)
        coupling = jnp.zeros((5, 2, PAIRS, NCELLS), jnp.float32)
        for face_index in range(6):
            beside = jnp.take_along_axis(extended, local_index[face_index][None, None, None], axis=4).reshape(5, 2, PAIRS, NCELLS)
            jacobian = off_jacobian[face_index].astype(jnp.float32)
            for comp_index in range(5):
                coupling = coupling + jacobian[:, comp_index, None, None, :] * beside[comp_index][None]
        spinning = jnp.stack([-angular * iterate[:, 1], angular * iterate[:, 0]], axis=1)
        residual_now = rhs_full - coupling - spinning
        update = jnp.zeros((5, 2, PAIRS, NCELLS), jnp.float32)
        for comp_index in range(5):
            update = update + diag_inverse[:, comp_index, None, None, :] * residual_now[comp_index][None]
        iterate = update
    return iterate
```

```python
import functools

import jax
import jax.numpy as jnp
from jax import lax
from jax.experimental import pallas as pl
from jax.experimental.pallas import tpu as pltpu
from jax.sharding import PartitionSpec as P

SWEEPS = 2
OFFSETS = (1, -1, 2, -2)
LANES = 128
MESH = pl.DeviceIdType.MESH
F32 = jnp.float32
BF16 = jnp.bfloat16


def iota(shape, axis):
    return lax.broadcasted_iota(jnp.int32, shape, axis)


def split(value):
    high = value.astype(BF16)
    return high, (value - high.astype(F32)).astype(BF16)


def dot_last(a, b):
    return lax.dot_general(a, b, (((1,), (1,)), ((), ())), preferred_element_type=F32)


def lane_pick(table, index):
    return jnp.take_along_axis(table, index, axis=1, mode="promise_in_bounds")


class Plan:
    def __init__(self, dom, rep, spline, face_dest, flow_rhs, send_list):
        self.dom, self.rep = dom, rep
        self.blocks = spline.shape[0]
        self.faces = face_dest.shape[0]
        self.own_faces = self.faces // rep
        self.pairs = flow_rhs.shape[2]
        self.comps = flow_rhs.shape[0]
        self.cells = flow_rhs.shape[3]
        self.halo = send_list.shape[1]
        self.part_rows = 2 * self.pairs
        self.rows = self.comps * self.part_rows
        self.row_pad = -(-self.rows // 8) * 8
        self.values = 2 * self.part_rows
        self.cap = 2 * self.faces // dom
        self.width = min(2 * LANES, self.cap)
        self.steps = self.cap // self.width
        count = self.values + 1
        while count * self.steps % 8:
            count += 1
        self.slot_rows = count * self.steps
        self.chunks = self.cells // LANES
        self.halo_chunks = self.halo // LANES
        self.face_chunks = self.faces // LANES


def kernel(
    pn,
    freq_ref,
    spline_ref,
    coeff_ref,
    dest_ref,
    cell_ref,
    weight_ref,
    flow_ref,
    prev_ref,
    diag_ref,
    jac_ref,
    neighbor_ref,
    send_ref,
    out_ref,
    part_buf,
    face_buf,
    slot_buf,
    left_buf,
    right_buf,
    pack_buf,
    recv_buf,
    add_left,
    add_right,
    wall_buf,
    field,
    ghost,
    halo_send,
    beside,
    jac,
    diag,
    weight,
    flow,
    iterate,
    coupled,
    rep_send_sem,
    rep_recv_sem,
    dom_send_sem,
    dom_recv_sem,
    halo_send_sem,
    halo_recv_sem,
):
    me_dom, me_rep = lax.axis_index("dom"), lax.axis_index("rep")
    n_ch, rows, rpad, width = pn.chunks, pn.rows, pn.row_pad, pn.part_rows
    groups = rpad // 8

    barrier = pltpu.get_barrier_semaphore()
    for offset in range(1, pn.rep):
        pl.semaphore_signal(
            barrier, inc=1, device_id=(me_dom, lax.rem(me_rep + offset, pn.rep)), device_id_type=MESH
        )

    def greet(offset, carry):
        pl.semaphore_signal(
            barrier, inc=1, device_id=(lax.rem(me_dom + offset, pn.dom), me_rep), device_id_type=MESH
        )
        return carry

    lax.fori_loop(1, pn.dom, greet, 0)

    row_id = iota((pn.rep * pn.values, LANES), 0)
    pair_id = row_id // pn.values * pn.pairs + row_id % pn.pairs
    scale = jnp.zeros(row_id.shape, F32)
    for pair in range(pn.rep * pn.pairs):
        scale = jnp.where(pair_id == pair, freq_ref[pair], scale)
    scale = jnp.where(row_id // pn.pairs % 2 == 0, -scale, scale)
    scale = jnp.where(row_id // width % 2 == 0, scale, 1.0)
    for block in range(pn.blocks):
        base = jnp.dot(coeff_ref[...], spline_ref[block], preferred_element_type=F32) * scale
        for peer in range(pn.rep):
            part_buf[peer, :, block * LANES : (block + 1) * LANES] = base[
                peer * pn.values : (peer + 1) * pn.values
            ]

    pl.semaphore_wait(barrier, pn.rep - 1 + pn.dom - 1)

    def rep_copy(offset):
        peer = lax.rem(me_rep + offset, pn.rep)
        return pltpu.make_async_remote_copy(
            src_ref=part_buf.at[peer],
            dst_ref=face_buf.at[me_rep],
            send_sem=rep_send_sem.at[offset],
            recv_sem=rep_recv_sem.at[offset],
            device_id=(me_dom, peer),
            device_id_type=MESH,
        )

    for offset in range(1, pn.rep):
        rep_copy(offset).start()
    face_buf[me_rep] = part_buf[me_rep]

    group = min(8, pn.dom)
    lines = pn.face_chunks
    tri = jnp.where(
        (iota((LANES, 2 * LANES), 1) >= LANES)
        | (iota((LANES, 2 * LANES), 0) <= iota((LANES, 2 * LANES), 1)),
        1.0,
        0.0,
    ).astype(BF16)
    size = group * lines
    above = jnp.where(
        (iota((size, size), 0) // lines == iota((size, size), 1) // lines)
        & (iota((size, size), 1) < iota((size, size), 0)),
        1.0,
        0.0,
    ).astype(BF16)
    dest = dest_ref[...]
    slots = jnp.zeros((lines, LANES), F32)
    for first in range(0, pn.dom, group):
        mask = jnp.concatenate(
            [jnp.where(dest == first + d, 1.0, 0.0) for d in range(group)], axis=0
        )
        counts = jnp.dot(mask.astype(BF16), tri, preferred_element_type=F32)
        before = jnp.dot(above, counts[:, LANES:].astype(BF16), preferred_element_type=F32)
        place = mask * (counts[:, :LANES] + before - 1.0)
        for d in range(group):
            part = slice(d * lines, (d + 1) * lines)
            slots = slots + place[part] + mask[part] * float((first + d) * pn.cap)
    slot_buf[...] = slots.astype(jnp.int32)

    def unfold(source, target, base):
        for tile in range(n_ch):
            target[pl.ds(base + tile, source.shape[0], stride=n_ch), :] = source[
                :, tile * LANES : (tile + 1) * LANES
            ]

    def spread_field():
        for row in range(rows):
            field[pl.ds(row, n_ch, stride=rpad), :] = iterate[row * n_ch : (row + 1) * n_ch]

    def pick(table, first_chunk, count, index, start):
        low, high = index % LANES, index // LANES
        picked = list(start)
        for chunk in range(count):
            here = high == first_chunk + chunk
            for g in range(groups):
                found = lane_pick(table[pl.ds(chunk * rpad + g * 8, 8), :], low)
                picked[g] = jnp.where(here, found, picked[g])
        return picked

    def wide_row(ref, row, tile):
        line = ref[row : row + 1, pl.ds(pl.multiple_of(tile * LANES, LANES), LANES)]
        return jnp.broadcast_to(line, (8, LANES))

    zeros = [jnp.zeros((8, LANES), F32)] * groups

    def halo_copy(sweep, block):
        return pltpu.make_async_remote_copy(
            src_ref=halo_send.at[sweep, block],
            dst_ref=ghost.at[sweep, block],
            send_sem=halo_send_sem.at[sweep, block],
            recv_sem=halo_recv_sem.at[sweep, block],
            device_id=(lax.rem(me_dom + OFFSETS[block] + pn.dom, pn.dom), me_rep),
            device_id_type=MESH,
        )

    def send_halo(sweep):
        for block in range(4):
            for half in range(pn.halo_chunks):
                found = pick(field, 0, n_ch, wide_row(send_ref, block, half), zeros)
                for g in range(groups):
                    halo_send[sweep, block, half * rpad + g * 8 : half * rpad + g * 8 + 8, :] = found[g]
            halo_copy(sweep, block).start()

    def beside_at(face, tile, g):
        count = min(8, rows - g * 8)
        return pl.ds((face * rows + g * 8) * n_ch + tile, count, stride=n_ch), count

    n_faces = neighbor_ref.shape[0]

    def gather_local():
        def body(face, tile, carry):
            found = pick(field, 0, n_ch, wide_row(neighbor_ref, face, tile), zeros)
            for g in range(groups):
                where, count = beside_at(face, tile, g)
                beside[where, :] = found[g][:count]
            return carry

        for face in range(n_faces):
            lax.fori_loop(0, n_ch, functools.partial(body, face), 0)

    def gather_ghost(sweep):
        for block in range(4):
            halo_copy(sweep, block).wait()

        def body(face, tile, carry):
            start = []
            for g in range(groups):
                where, count = beside_at(face, tile, g)
                value = beside[where, :]
                if count < 8:
                    value = jnp.concatenate([value, jnp.zeros((8 - count, LANES), F32)], axis=0)
                start.append(value)
            index = wide_row(neighbor_ref, face, tile)
            for block in range(4):
                start = pick(
                    ghost.at[sweep, block], n_ch + block * pn.halo_chunks, pn.halo_chunks, index, start
                )
            for g in range(groups):
                where, count = beside_at(face, tile, g)
                beside[where, :] = start[g][:count]
            return carry

        for face in range(n_faces):
            lax.fori_loop(0, n_ch, functools.partial(body, face), 0)

    def line(ref, index):
        return ref[pl.ds(pl.multiple_of(index * n_ch, n_ch), n_ch), :]

    def couple():
        def body(e, carry):
            total = [jnp.zeros((n_ch, LANES), F32)] * width
            for face in range(n_faces):
                for g in range(pn.comps):
                    entry = line(jac, (face * pn.comps + e) * pn.comps + g)
                    for k in range(width):
                        total[k] = total[k] + entry * line(beside, face * rows + g * width + k)
            for k in range(width):
                coupled[pl.ds(pl.multiple_of((e * width + k) * n_ch, n_ch), n_ch), :] = total[k]
            return carry

        lax.fori_loop(0, pn.comps, body, 0)

    def update():
        own = [freq_ref[me_rep * pn.pairs + p] for p in range(pn.pairs)]
        for k in range(width):
            part, pair = k // pn.pairs, k % pn.pairs
            turned = (1 - part) * pn.pairs + pair
            sign = own[pair] if part == 0 else -own[pair]
            residual = []
            for g in range(pn.comps):
                row = g * width + k
                residual.append(
                    line(flow, row) - line(coupled, row) + sign * line(iterate, g * width + turned)
                )
            for e in range(pn.comps):
                total = line(diag, e * pn.comps) * residual[0]
                for g in range(1, pn.comps):
                    total = total + line(diag, e * pn.comps + g) * residual[g]
                row = e * width + k
                coupled[row * n_ch : (row + 1) * n_ch, :] = total
        for row in range(rows):
            iterate[row * n_ch : (row + 1) * n_ch, :] = line(coupled, row)

    for e in range(pn.comps):
        for r in range(2):
            unfold(prev_ref[e, r], iterate, (e * width + r * pn.pairs) * n_ch)
    spread_field()
    send_halo(0)

    for offset in range(1, pn.rep):
        rep_copy(offset).wait()

    per = 4 if lines % 4 == 0 else 1
    n_slot = pn.dom * pn.slot_rows
    pack_flat = pack_buf
    for d in range(pn.dom):
        pack_buf[d] = jnp.zeros((pn.slot_rows, pn.width), F32)

    def pack(turn, carry):
        for c in range(per):
            chunk = turn * per + c
            lanes = slice(c * LANES, (c + 1) * LANES)
            slot = slot_buf[pl.ds(chunk, 1), :]
            owner = chunk // pn.blocks
            column = pl.multiple_of(chunk % pn.blocks * LANES, LANES)
            value = face_buf[owner, :, pl.ds(column, LANES)]
            cell = cell_ref[pl.ds(chunk, 1), :].astype(F32)
            low = jnp.broadcast_to(slot % pn.width, (pn.width, LANES))
            right_buf[:, lanes] = jnp.where(low == iota((pn.width, LANES), 0), 1.0, 0.0).astype(BF16)
            high = jnp.broadcast_to(slot // pn.width, (8, LANES))
            sub = iota((8, LANES), 0)
            tiles = []
            for tile in range(pn.slot_rows // 8):
                row = jnp.zeros((8, LANES), F32)
                for v in range(pn.values + 1):
                    source = value[v : v + 1] if v < pn.values else cell
                    low_row, top_row = v * pn.steps - tile * 8, (v + 1) * pn.steps - tile * 8
                    if top_row <= 0 or low_row >= 8:
                        continue
                    inside = (sub >= low_row) & (sub < top_row)
                    row = jnp.where(inside, jnp.broadcast_to(source, (8, LANES)), row)
                tiles.append(row)
            parts = [split(t) for t in tiles]
            parts = [(a.astype(F32), b.astype(F32)) for a, b in parts]
            halves = ([], [])
            for d in range(pn.dom):
                for tile in range(pn.slot_rows // 8):
                    step = (sub + tile * 8) % pn.steps
                    here = high == d * pn.steps + step
                    for half in range(2):
                        halves[half].append(jnp.where(here, parts[tile][half], 0.0))
            left_buf[0:n_slot, lanes] = jnp.concatenate(halves[0], axis=0).astype(BF16)
            left_buf[n_slot : 2 * n_slot, lanes] = jnp.concatenate(halves[1], axis=0).astype(BF16)
        found = dot_last(left_buf[...], right_buf[...])
        for d in range(pn.dom):
            a, b = d * pn.slot_rows, n_slot + d * pn.slot_rows
            pack_buf[d] += found[a : a + pn.slot_rows] + found[b : b + pn.slot_rows]
        return carry

    lax.fori_loop(0, lines // per, pack, 0)

    def dom_copy(offset):
        target = lax.rem(me_dom + offset, pn.dom)
        return pltpu.make_async_remote_copy(
            src_ref=pack_buf.at[target],
            dst_ref=recv_buf.at[offset],
            send_sem=dom_send_sem.at[offset],
            recv_sem=dom_recv_sem.at[offset],
            device_id=(target, me_rep),
            device_id_type=MESH,
        )

    def send_faces(offset, carry):
        dom_copy(offset).start()
        return carry

    lax.fori_loop(1, pn.dom, send_faces, 0)
    recv_buf[0] = pack_buf[me_dom]

    def unfold_jac(index, carry):
        unfold(jac_ref[index].astype(F32), jac, index * (pn.comps * n_ch))
        return carry

    lax.fori_loop(0, n_faces * pn.comps, unfold_jac, 0)
    for e in range(pn.comps):
        unfold(diag_ref[e], diag, e * pn.comps * n_ch)
        unfold(weight_ref[e], weight, e * 2 * n_ch)
        for r in range(2):
            unfold(flow_ref[e, r], flow, (e * width + r * pn.pairs) * n_ch)
    gather_local()
    gather_ghost(0)
    couple()

    wall_buf[...] = jnp.zeros(wall_buf.shape, F32)
    half_rows = pn.values * n_ch

    def add_faces(offset):
        for step in range(pn.steps):
            for part in range(pn.width // LANES):
                place = step * pn.width + part * LANES
                lanes = slice(part * LANES, (part + 1) * LANES)
                row = pn.values * pn.steps + step
                cell = recv_buf[offset, row : row + 1, lanes].astype(jnp.int32)
                low = jnp.broadcast_to(cell % LANES, (LANES, LANES))
                add_right[:, place : place + LANES] = jnp.where(
                    low == iota((LANES, LANES), 0), 1.0, 0.0
                ).astype(BF16)
                here = jnp.broadcast_to(cell // LANES, (n_ch, LANES)) == iota((n_ch, LANES), 0)
                for v in range(pn.values):
                    row = v * pn.steps + step
                    value = jnp.broadcast_to(recv_buf[offset, row : row + 1, lanes], (n_ch, LANES))
                    first, second = split(jnp.where(here, value, 0.0))
                    add_left[v * n_ch : (v + 1) * n_ch, place : place + LANES] = first
                    add_left[
                        half_rows + v * n_ch : half_rows + (v + 1) * n_ch, place : place + LANES
                    ] = second
        found = dot_last(add_left[...], add_right[...])
        wall_buf[...] += found[:half_rows] + found[half_rows:]

    add_faces(0)

    def receive(offset, carry):
        dom_copy(offset).wait()
        add_faces(offset)
        return carry

    lax.fori_loop(1, pn.dom, receive, 0)

    for e in range(pn.comps):
        first, second = line(weight, 2 * e), line(weight, 2 * e + 1)
        for k in range(width):
            row = e * width + k
            flow[row * n_ch : (row + 1) * n_ch, :] = (
                line(flow, row) + first * line(wall_buf, k) + second * line(wall_buf, width + k)
            )

    update()
    for sweep in range(1, SWEEPS):
        spread_field()
        send_halo(sweep)
        gather_local()
        gather_ghost(sweep)
        couple()
        update()

    for e in range(pn.comps):
        for r in range(2):
            for tile in range(n_ch):
                start = (e * width + r * pn.pairs) * n_ch + tile
                out_ref[e, r, :, tile * LANES : (tile + 1) * LANES] = iterate[
                    pl.ds(start, pn.pairs, stride=n_ch), :
                ]


def shards(
    dom,
    rep,
    spline_blocks,
    modal_coeff,
    frequency,
    face_dest,
    face_cell,
    wall_weight,
    flow_rhs,
    previous,
    diag_inverse,
    off_jacobian,
    neighbor,
    send_list,
):
    pn = Plan(dom, rep, spline_blocks, face_dest, flow_rhs, send_list)
    modes = modal_coeff.shape[0]
    turned = jnp.transpose(modal_coeff.reshape(modes, 2, rep, pn.pairs), (2, 1, 3, 0))
    both = jnp.stack([turned[:, ::-1], turned], axis=1)
    same = jnp.eye(2, dtype=BF16)[None, :, None, None, :, None]
    coeff = (both[:, :, :, :, None, :] * same).reshape(rep * pn.values, 2 * modes)
    n_faces = neighbor.shape[0]
    lines = pn.face_chunks
    per = 4 if lines % 4 == 0 else 1
    vmem = pl.BlockSpec(memory_space=pltpu.VMEM)
    return pl.pallas_call(
        functools.partial(kernel, pn),
        out_shape=jax.ShapeDtypeStruct(previous.shape, F32),
        in_specs=[pl.BlockSpec(memory_space=pltpu.SMEM)] + [vmem] * 11,
        out_specs=vmem,
        scratch_shapes=[
            pltpu.VMEM((rep, pn.values, pn.own_faces), F32),
            pltpu.VMEM((rep, pn.values, pn.own_faces), F32),
            pltpu.VMEM((lines, LANES), jnp.int32),
            pltpu.VMEM((2 * dom * pn.slot_rows, per * LANES), BF16),
            pltpu.VMEM((pn.width, per * LANES), BF16),
            pltpu.VMEM((dom, pn.slot_rows, pn.width), F32),
            pltpu.VMEM((dom, pn.slot_rows, pn.width), F32),
            pltpu.VMEM((2 * pn.values * pn.chunks, pn.cap), BF16),
            pltpu.VMEM((LANES, pn.cap), BF16),
            pltpu.VMEM((pn.values * pn.chunks, LANES), F32),
            pltpu.VMEM((pn.chunks * pn.row_pad, LANES), F32),
            pltpu.VMEM((SWEEPS, 4, pn.halo_chunks * pn.row_pad, LANES), F32),
            pltpu.VMEM((SWEEPS, 4, pn.halo_chunks * pn.row_pad, LANES), F32),
            pltpu.VMEM((n_faces * pn.rows * pn.chunks, LANES), F32),
            pltpu.VMEM((n_faces * pn.comps * pn.comps * pn.chunks, LANES), F32),
            pltpu.VMEM((pn.comps * pn.comps * pn.chunks, LANES), F32),
            pltpu.VMEM((pn.comps * 2 * pn.chunks, LANES), F32),
            pltpu.VMEM((pn.rows * pn.chunks, LANES), F32),
            pltpu.VMEM((pn.rows * pn.chunks, LANES), F32),
            pltpu.VMEM((pn.rows * pn.chunks, LANES), F32),
            pltpu.SemaphoreType.DMA((rep,)),
            pltpu.SemaphoreType.DMA((rep,)),
            pltpu.SemaphoreType.DMA((dom,)),
            pltpu.SemaphoreType.DMA((dom,)),
            pltpu.SemaphoreType.DMA((SWEEPS, 4)),
            pltpu.SemaphoreType.DMA((SWEEPS, 4)),
        ],
        compiler_params=pltpu.CompilerParams(
            collective_id=0, has_side_effects=True, vmem_limit_bytes=48 * 1024 * 1024
        ),
    )(
        frequency,
        spline_blocks.reshape(pn.blocks, 2 * modes, LANES),
        coeff,
        face_dest.reshape(lines, LANES),
        face_cell.reshape(lines, LANES),
        wall_weight,
        flow_rhs,
        previous,
        diag_inverse,
        off_jacobian.reshape(n_faces * pn.comps, pn.comps, pn.cells),
        neighbor,
        send_list,
    )


def solution(mesh):
    return jax.shard_map(
        functools.partial(shards, mesh.shape["dom"], mesh.shape["rep"]),
        mesh=mesh,
        in_specs=(
            P(("dom", "rep"), None, None, None),
            P(),
            P(),
            P("dom", None),
            P("dom"),
            P(None, None, "dom"),
            P(None, None, "rep", "dom"),
            P(None, None, "rep", "dom"),
            P(None, None, "dom"),
            P(None, None, None, "dom"),
            P(None, "dom"),
            P(None, "dom"),
        ),
        out_specs=P(None, None, "rep", "dom"),
        check_vma=False,
    )
```

```python
import functools

import jax
import jax.numpy as jnp
from jax import lax
from jax.experimental import pallas as pl
from jax.experimental.pallas import tpu as pltpu
from jax.sharding import PartitionSpec as P

SWEEPS = 2
OFFSETS = (1, -1, 2, -2)
LANES = 128
MESH = pl.DeviceIdType.MESH
F32 = jnp.float32
BF16 = jnp.bfloat16


def iota(shape, axis):
    return lax.broadcasted_iota(jnp.int32, shape, axis)


def remainder(value, size):
    return value & (size - 1) if size & (size - 1) == 0 else value % size


def quotient(value, size):
    return value >> (size.bit_length() - 1) if size & (size - 1) == 0 else value // size


def split(value):
    high = value.astype(BF16)
    return high, (value - high.astype(F32)).astype(BF16)


def dot_last(a, b):
    return lax.dot_general(a, b, (((1,), (1,)), ((), ())), preferred_element_type=F32)


class Plan:
    def __init__(self, dom, rep, spline, face_dest, flow_rhs, send_list):
        self.dom, self.rep = dom, rep
        self.blocks = spline.shape[0]
        self.faces = face_dest.shape[0]
        self.own_faces = self.faces // rep
        self.pairs = flow_rhs.shape[2]
        self.comps = flow_rhs.shape[0]
        self.cells = flow_rhs.shape[3]
        self.halo = send_list.shape[1]
        self.part_rows = 2 * self.pairs
        self.rows = self.comps * self.part_rows
        self.row_pad = -(-self.rows // 8) * 8
        self.values = 2 * self.part_rows
        self.cap = 2 * self.faces // dom
        self.width = min(2 * LANES, self.cap)
        self.steps = self.cap // self.width
        count = self.values + 1
        while count * self.steps % 8:
            count += 1
        self.slot_rows = count * self.steps
        self.chunks = self.cells // LANES
        self.wide = min(2 * LANES, self.halo)
        self.face_chunks = self.faces // LANES


def kernel(
    pn,
    freq_ref,
    spline_ref,
    coeff_ref,
    dest_ref,
    cell_ref,
    weight_ref,
    flow_ref,
    prev_ref,
    diag_ref,
    jac_ref,
    neighbor_ref,
    send_ref,
    out_ref,
    part_buf,
    face_buf,
    slot_buf,
    left_buf,
    right_buf,
    pack_buf,
    recv_buf,
    add_left,
    add_right,
    wall_buf,
    field,
    table,
    table_far,
    hot_send,
    hot_near,
    high_buf,
    near,
    ghost,
    halo_send,
    beside,
    jac,
    diag,
    weight,
    flow,
    iterate,
    coupled,
    rep_send_sem,
    rep_recv_sem,
    dom_send_sem,
    dom_recv_sem,
    halo_send_sem,
    halo_recv_sem,
):
    me_dom, me_rep = lax.axis_index("dom"), lax.axis_index("rep")
    n_ch, rows, rpad, width = pn.chunks, pn.rows, pn.row_pad, pn.part_rows
    groups = rpad // 8

    barrier = pltpu.get_barrier_semaphore()
    for offset in range(1, pn.rep):
        pl.semaphore_signal(
            barrier, inc=1, device_id=(me_dom, lax.rem(me_rep + offset, pn.rep)), device_id_type=MESH
        )

    def greet(offset, carry):
        pl.semaphore_signal(
            barrier, inc=1, device_id=(lax.rem(me_dom + offset, pn.dom), me_rep), device_id_type=MESH
        )
        return carry

    lax.fori_loop(1, pn.dom, greet, 0)

    row_id = iota((pn.rep * pn.values, LANES), 0)
    pair_id = row_id // pn.values * pn.pairs + row_id % pn.pairs
    scale = jnp.zeros(row_id.shape, F32)
    for pair in range(pn.rep * pn.pairs):
        scale = jnp.where(pair_id == pair, freq_ref[pair], scale)
    scale = jnp.where(row_id // pn.pairs % 2 == 0, -scale, scale)
    scale = jnp.where(row_id // width % 2 == 0, scale, 1.0)
    for block in range(pn.blocks):
        base = jnp.dot(coeff_ref[...], spline_ref[block], preferred_element_type=F32) * scale
        for peer in range(pn.rep):
            part_buf[peer, :, block * LANES : (block + 1) * LANES] = base[
                peer * pn.values : (peer + 1) * pn.values
            ]

    pl.semaphore_wait(barrier, pn.rep - 1 + pn.dom - 1)

    def rep_copy(offset):
        peer = lax.rem(me_rep + offset, pn.rep)
        return pltpu.make_async_remote_copy(
            src_ref=part_buf.at[peer],
            dst_ref=face_buf.at[me_rep],
            send_sem=rep_send_sem.at[offset],
            recv_sem=rep_recv_sem.at[offset],
            device_id=(me_dom, peer),
            device_id_type=MESH,
        )

    for offset in range(1, pn.rep):
        rep_copy(offset).start()
    face_buf[me_rep] = part_buf[me_rep]

    group = min(8, pn.dom)
    lines = pn.face_chunks
    tri = jnp.where(
        (iota((LANES, 2 * LANES), 1) >= LANES)
        | (iota((LANES, 2 * LANES), 0) <= iota((LANES, 2 * LANES), 1)),
        1.0,
        0.0,
    ).astype(BF16)
    size = group * lines
    above = jnp.where(
        (iota((size, size), 0) // lines == iota((size, size), 1) // lines)
        & (iota((size, size), 1) < iota((size, size), 0)),
        1.0,
        0.0,
    ).astype(BF16)
    dest = dest_ref[...]
    slots = jnp.zeros((lines, LANES), F32)
    for first in range(0, pn.dom, group):
        mask = jnp.concatenate(
            [jnp.where(dest == first + d, 1.0, 0.0) for d in range(group)], axis=0
        )
        counts = jnp.dot(mask.astype(BF16), tri, preferred_element_type=F32)
        before = jnp.dot(above, counts[:, LANES:].astype(BF16), preferred_element_type=F32)
        place = mask * (counts[:, :LANES] + before - 1.0)
        for d in range(group):
            part = slice(d * lines, (d + 1) * lines)
            slots = slots + place[part] + mask[part] * float((first + d) * pn.cap)
    slot_buf[...] = slots.astype(jnp.int32)

    def unfold(source, target, base):
        for tile in range(n_ch):
            target[pl.ds(base + tile, source.shape[0], stride=n_ch), :] = source[
                :, tile * LANES : (tile + 1) * LANES
            ]

    wide, n_wide = pn.wide, pn.cells // pn.wide
    per_wide = wide // LANES
    n_faces = neighbor_ref.shape[0]

    def spread_field():
        for row in range(rows):
            field[pl.ds(row, n_ch, stride=rpad), :] = iterate[row * n_ch : (row + 1) * n_ch]
        blocks = [
            jnp.concatenate(
                [
                    field[chunk * rpad : (chunk + 1) * rpad, :]
                    for chunk in range(c * per_wide, (c + 1) * per_wide)
                ],
                axis=1,
            )
            for c in range(n_wide)
        ]
        table[:, :wide], table[:, wide:] = split(jnp.concatenate(blocks, axis=0))

    def pick(parts, first_chunk, count, hot, high, start):
        found = jnp.dot(parts, jnp.concatenate([hot, hot], axis=0), preferred_element_type=F32)
        picked = list(start)
        for chunk in range(count):
            here = high == first_chunk + chunk
            for g in range(groups):
                at = chunk * rpad + g * 8
                picked[g] = jnp.where(here, found[at : at + 8], picked[g])
        return picked

    def one_hot(low, target):
        both = jnp.concatenate([low, low], axis=0)

        def body(turn, carry):
            first = pl.multiple_of(turn * 16, 16)
            target[pl.ds(first, 16), :] = jnp.where(
                both == iota(both.shape, 0) + first, 1.0, 0.0
            ).astype(BF16)
            return carry

        lax.fori_loop(0, wide // 16, body, 0)

    def halo_copy(sweep, block):
        return pltpu.make_async_remote_copy(
            src_ref=halo_send.at[sweep, block],
            dst_ref=ghost.at[sweep, block],
            send_sem=halo_send_sem.at[sweep, block],
            recv_sem=halo_recv_sem.at[sweep, block],
            device_id=(lax.rem(me_dom + OFFSETS[block] + pn.dom, pn.dom), me_rep),
            device_id_type=MESH,
        )

    def send_halo(sweep):
        for block in range(4):
            index = jnp.broadcast_to(send_ref[block : block + 1, :], (8, pn.halo))
            zeros = [jnp.zeros((8, pn.halo), F32)] * groups
            found = pick(table[...], 0, n_wide, hot_send[block], quotient(index, wide), zeros)
            for g in range(groups):
                halo_send[sweep, block, g * 8 : g * 8 + 8, :] = found[g]
            halo_copy(sweep, block).start()

    def gather_local():
        def body(face, carry):
            high = high_buf[face]
            zeros = [jnp.zeros(high.shape, F32)] * groups
            found = pick(table[...], 0, n_wide, hot_near[face], high, zeros)
            for g in range(groups):
                near[face, g * 8 : g * 8 + 8, :] = found[g]
            return carry

        lax.fori_loop(0, n_faces, body, 0)

    n_ghost = pn.halo // wide

    def gather_ghost(sweep):
        for block in range(4):
            halo_copy(sweep, block).wait()
        blocks = []
        for chunk in range(4 * n_ghost):
            lane = chunk % n_ghost * wide
            blocks.append(ghost[sweep, chunk // n_ghost, :, lane : lane + wide])
        table_far[:, :wide], table_far[:, wide:] = split(jnp.concatenate(blocks, axis=0))

        def body(face, carry):
            start = [near[face, g * 8 : g * 8 + 8, :] for g in range(groups)]
            found = pick(table_far[...], n_wide, 4 * n_ghost, hot_near[face], high_buf[face], start)
            for g in range(groups):
                count = min(8, rows - g * 8)
                for tile in range(n_ch):
                    where = pl.ds((face * rows + g * 8) * n_ch + tile, count, stride=n_ch)
                    beside[where, :] = found[g][:count, tile * LANES : (tile + 1) * LANES]
            return carry

        lax.fori_loop(0, n_faces, body, 0)

    def line(ref, index):
        return ref[pl.ds(pl.multiple_of(index * n_ch, n_ch), n_ch), :]

    def couple():
        def body(e, carry):
            total = [jnp.zeros((n_ch, LANES), F32)] * width
            for face in range(n_faces):
                for g in range(pn.comps):
                    entry = line(jac, (e * pn.comps + g) * n_faces + face)
                    for k in range(width):
                        total[k] = total[k] + entry * line(beside, face * rows + g * width + k)
            for k in range(width):
                coupled[pl.ds(pl.multiple_of((e * width + k) * n_ch, n_ch), n_ch), :] = total[k]
            return carry

        lax.fori_loop(0, pn.comps, body, 0)

    def update():
        own = [freq_ref[me_rep * pn.pairs + p] for p in range(pn.pairs)]
        for k in range(width):
            part, pair = k // pn.pairs, k % pn.pairs
            turned = (1 - part) * pn.pairs + pair
            sign = own[pair] if part == 0 else -own[pair]
            residual = []
            for g in range(pn.comps):
                row = g * width + k
                residual.append(
                    line(flow, row) - line(coupled, row) + sign * line(iterate, g * width + turned)
                )
            for e in range(pn.comps):
                total = line(diag, e * pn.comps) * residual[0]
                for g in range(1, pn.comps):
                    total = total + line(diag, e * pn.comps + g) * residual[g]
                row = e * width + k
                coupled[row * n_ch : (row + 1) * n_ch, :] = total
        for row in range(rows):
            iterate[row * n_ch : (row + 1) * n_ch, :] = line(coupled, row)

    for e in range(pn.comps):
        for r in range(2):
            unfold(prev_ref[e, r], iterate, (e * width + r * pn.pairs) * n_ch)
    field[...] = jnp.zeros(field.shape, F32)
    spread_field()
    for block in range(4):
        index = jnp.broadcast_to(send_ref[block : block + 1, :], (8, pn.halo))
        one_hot(remainder(index, wide), hot_send.at[block])
    send_halo(0)

    for offset in range(1, pn.rep):
        rep_copy(offset).wait()

    per = 8 if lines % 8 == 0 else 1
    n_slot = pn.dom * pn.slot_rows
    for d in range(pn.dom):
        pack_buf[d] = jnp.zeros((pn.slot_rows, pn.width), F32)

    def pack(turn, carry):
        for c in range(per):
            chunk = turn * per + c
            lanes = slice(c * LANES, (c + 1) * LANES)
            slot = slot_buf[pl.ds(chunk, 1), :]
            owner = chunk // pn.blocks
            column = pl.multiple_of(chunk % pn.blocks * LANES, LANES)
            value = face_buf[owner, :, pl.ds(column, LANES)]
            cell = cell_ref[pl.ds(chunk, 1), :].astype(F32)
            low = jnp.broadcast_to(remainder(slot, pn.width), (pn.width, LANES))
            right_buf[:, lanes] = jnp.where(low == iota((pn.width, LANES), 0), 1.0, 0.0).astype(BF16)
            high = jnp.broadcast_to(quotient(slot, pn.width), (8, LANES))
            sub = iota((8, LANES), 0)
            tiles = []
            for tile in range(pn.slot_rows // 8):
                row = jnp.zeros((8, LANES), F32)
                for v in range(pn.values + 1):
                    source = value[v : v + 1] if v < pn.values else cell
                    low_row, top_row = v * pn.steps - tile * 8, (v + 1) * pn.steps - tile * 8
                    if top_row <= 0 or low_row >= 8:
                        continue
                    inside = (sub >= low_row) & (sub < top_row)
                    row = jnp.where(inside, jnp.broadcast_to(source, (8, LANES)), row)
                tiles.append(row)
            parts = [split(t) for t in tiles]
            parts = [(a.astype(F32), b.astype(F32)) for a, b in parts]
            halves = ([], [])
            for d in range(pn.dom):
                for tile in range(pn.slot_rows // 8):
                    step = remainder(sub + tile * 8, pn.steps)
                    here = high == d * pn.steps + step
                    for half in range(2):
                        halves[half].append(jnp.where(here, parts[tile][half], 0.0))
            left_buf[0:n_slot, lanes] = jnp.concatenate(halves[0], axis=0).astype(BF16)
            left_buf[n_slot : 2 * n_slot, lanes] = jnp.concatenate(halves[1], axis=0).astype(BF16)
        found = dot_last(left_buf[...], right_buf[...])
        for d in range(pn.dom):
            a, b = d * pn.slot_rows, n_slot + d * pn.slot_rows
            pack_buf[d] += found[a : a + pn.slot_rows] + found[b : b + pn.slot_rows]
        return carry

    lax.fori_loop(0, lines // per, pack, 0)

    def dom_copy(offset):
        target = lax.rem(me_dom + offset, pn.dom)
        return pltpu.make_async_remote_copy(
            src_ref=pack_buf.at[target],
            dst_ref=recv_buf.at[offset],
            send_sem=dom_send_sem.at[offset],
            recv_sem=dom_recv_sem.at[offset],
            device_id=(target, me_rep),
            device_id_type=MESH,
        )

    def send_faces(offset, carry):
        dom_copy(offset).start()
        return carry

    lax.fori_loop(1, pn.dom, send_faces, 0)
    recv_buf[0] = pack_buf[me_dom]

    def unfold_jac(index, carry):
        unfold(jac_ref[index].astype(F32), jac, index * (n_faces * n_ch))
        return carry

    lax.fori_loop(0, pn.comps * pn.comps, unfold_jac, 0)
    for face in range(n_faces):
        index = jnp.broadcast_to(neighbor_ref[face : face + 1, :], (8, pn.cells))
        high_buf[face] = quotient(index, wide)
        one_hot(remainder(index, wide), hot_near.at[face])
    for e in range(pn.comps):
        unfold(diag_ref[e], diag, e * pn.comps * n_ch)
        unfold(weight_ref[e], weight, e * 2 * n_ch)
        for r in range(2):
            unfold(flow_ref[e, r], flow, (e * width + r * pn.pairs) * n_ch)
    gather_local()
    gather_ghost(0)
    couple()

    wall_buf[...] = jnp.zeros(wall_buf.shape, F32)
    half_rows = pn.values * n_ch

    def add_faces(offset):
        for step in range(pn.steps):
            for part in range(pn.width // LANES):
                place = step * pn.width + part * LANES
                lanes = slice(part * LANES, (part + 1) * LANES)
                row = pn.values * pn.steps + step
                cell = recv_buf[offset, row : row + 1, lanes].astype(jnp.int32)
                low = jnp.broadcast_to(remainder(cell, LANES), (LANES, LANES))
                add_right[:, place : place + LANES] = jnp.where(
                    low == iota((LANES, LANES), 0), 1.0, 0.0
                ).astype(BF16)
                here = jnp.broadcast_to(quotient(cell, LANES), (n_ch, LANES)) == iota((n_ch, LANES), 0)
                for v in range(pn.values):
                    row = v * pn.steps + step
                    value = jnp.broadcast_to(recv_buf[offset, row : row + 1, lanes], (n_ch, LANES))
                    first, second = split(jnp.where(here, value, 0.0))
                    add_left[v * n_ch : (v + 1) * n_ch, place : place + LANES] = first
                    add_left[
                        half_rows + v * n_ch : half_rows + (v + 1) * n_ch, place : place + LANES
                    ] = second
        found = dot_last(add_left[...], add_right[...])
        wall_buf[...] += found[:half_rows] + found[half_rows:]

    add_faces(0)

    def receive(offset, carry):
        dom_copy(offset).wait()
        add_faces(offset)
        return carry

    lax.fori_loop(1, pn.dom, receive, 0)

    for e in range(pn.comps):
        first, second = line(weight, 2 * e), line(weight, 2 * e + 1)
        for k in range(width):
            row = e * width + k
            flow[row * n_ch : (row + 1) * n_ch, :] = (
                line(flow, row) + first * line(wall_buf, k) + second * line(wall_buf, width + k)
            )

    update()
    for sweep in range(1, SWEEPS):
        spread_field()
        send_halo(sweep)
        gather_local()
        gather_ghost(sweep)
        couple()
        update()

    for e in range(pn.comps):
        for r in range(2):
            for tile in range(n_ch):
                start = (e * width + r * pn.pairs) * n_ch + tile
                out_ref[e, r, :, tile * LANES : (tile + 1) * LANES] = iterate[
                    pl.ds(start, pn.pairs, stride=n_ch), :
                ]


def shards(
    dom,
    rep,
    spline_blocks,
    modal_coeff,
    frequency,
    face_dest,
    face_cell,
    wall_weight,
    flow_rhs,
    previous,
    diag_inverse,
    off_jacobian,
    neighbor,
    send_list,
):
    pn = Plan(dom, rep, spline_blocks, face_dest, flow_rhs, send_list)
    modes = modal_coeff.shape[0]
    turned = jnp.transpose(modal_coeff.reshape(modes, 2, rep, pn.pairs), (2, 1, 3, 0))
    both = jnp.stack([turned[:, ::-1], turned], axis=1)
    same = jnp.eye(2, dtype=BF16)[None, :, None, None, :, None]
    coeff = (both[:, :, :, :, None, :] * same).reshape(rep * pn.values, 2 * modes)
    n_faces = neighbor.shape[0]
    lines = pn.face_chunks
    per = 8 if lines % 8 == 0 else 1
    vmem = pl.BlockSpec(memory_space=pltpu.VMEM)
    return pl.pallas_call(
        functools.partial(kernel, pn),
        out_shape=jax.ShapeDtypeStruct(previous.shape, F32),
        in_specs=[pl.BlockSpec(memory_space=pltpu.SMEM)] + [vmem] * 11,
        out_specs=vmem,
        scratch_shapes=[
            pltpu.VMEM((rep, pn.values, pn.own_faces), F32),
            pltpu.VMEM((rep, pn.values, pn.own_faces), F32),
            pltpu.VMEM((lines, LANES), jnp.int32),
            pltpu.VMEM((2 * dom * pn.slot_rows, per * LANES), BF16),
            pltpu.VMEM((pn.width, per * LANES), BF16),
            pltpu.VMEM((dom, pn.slot_rows, pn.width), F32),
            pltpu.VMEM((dom, pn.slot_rows, pn.width), F32),
            pltpu.VMEM((2 * pn.values * pn.chunks, pn.cap), BF16),
            pltpu.VMEM((LANES, pn.cap), BF16),
            pltpu.VMEM((pn.values * pn.chunks, LANES), F32),
            pltpu.VMEM((pn.chunks * pn.row_pad, LANES), F32),
            pltpu.VMEM((pn.cells // pn.wide * pn.row_pad, 2 * pn.wide), BF16),
            pltpu.VMEM((4 * pn.halo // pn.wide * pn.row_pad, 2 * pn.wide), BF16),
            pltpu.VMEM((4, pn.wide, pn.halo), BF16),
            pltpu.VMEM((n_faces, pn.wide, pn.cells), BF16),
            pltpu.VMEM((n_faces, 8, pn.cells), jnp.int32),
            pltpu.VMEM((n_faces, pn.row_pad, pn.cells), F32),
            pltpu.VMEM((SWEEPS, 4, pn.row_pad, pn.halo), F32),
            pltpu.VMEM((SWEEPS, 4, pn.row_pad, pn.halo), F32),
            pltpu.VMEM((n_faces * pn.rows * pn.chunks, LANES), F32),
            pltpu.VMEM((n_faces * pn.comps * pn.comps * pn.chunks, LANES), F32),
            pltpu.VMEM((pn.comps * pn.comps * pn.chunks, LANES), F32),
            pltpu.VMEM((pn.comps * 2 * pn.chunks, LANES), F32),
            pltpu.VMEM((pn.rows * pn.chunks, LANES), F32),
            pltpu.VMEM((pn.rows * pn.chunks, LANES), F32),
            pltpu.VMEM((pn.rows * pn.chunks, LANES), F32),
            pltpu.SemaphoreType.DMA((rep,)),
            pltpu.SemaphoreType.DMA((rep,)),
            pltpu.SemaphoreType.DMA((dom,)),
            pltpu.SemaphoreType.DMA((dom,)),
            pltpu.SemaphoreType.DMA((SWEEPS, 4)),
            pltpu.SemaphoreType.DMA((SWEEPS, 4)),
        ],
        compiler_params=pltpu.CompilerParams(
            collective_id=0, has_side_effects=True, vmem_limit_bytes=48 * 1024 * 1024
        ),
    )(
        frequency,
        spline_blocks.reshape(pn.blocks, 2 * modes, LANES),
        coeff,
        face_dest.reshape(lines, LANES),
        face_cell.reshape(lines, LANES),
        wall_weight,
        flow_rhs,
        previous,
        diag_inverse,
        jnp.transpose(off_jacobian, (1, 2, 0, 3)).reshape(pn.comps * pn.comps, n_faces, pn.cells),
        neighbor,
        send_list,
    )


def solution(mesh):
    return jax.shard_map(
        functools.partial(shards, mesh.shape["dom"], mesh.shape["rep"]),
        mesh=mesh,
        in_specs=(
            P(("dom", "rep"), None, None, None),
            P(),
            P(),
            P("dom", None),
            P("dom"),
            P(None, None, "dom"),
            P(None, None, "rep", "dom"),
            P(None, None, "rep", "dom"),
            P(None, None, "dom"),
            P(None, None, None, "dom"),
            P(None, "dom"),
            P(None, "dom"),
        ),
        out_specs=P(None, None, "rep", "dom"),
        check_vma=False,
    )
```

```python
import functools

import jax
import jax.numpy as jnp
from jax import lax
from jax.experimental import pallas as pl
from jax.experimental.pallas import tpu as pltpu
from jax.sharding import PartitionSpec as P

SWEEPS = 2
OFFSETS = (1, -1, 2, -2)
LANES = 128
MESH = pl.DeviceIdType.MESH
F32 = jnp.float32
BF16 = jnp.bfloat16


def iota(shape, axis):
    return lax.broadcasted_iota(jnp.int32, shape, axis)


def remainder(value, size):
    return value & (size - 1) if size & (size - 1) == 0 else value % size


def quotient(value, size):
    return value >> (size.bit_length() - 1) if size & (size - 1) == 0 else value // size


def split(value):
    high = value.astype(BF16)
    return high, (value - high.astype(F32)).astype(BF16)


def dot_last(a, b):
    return lax.dot_general(a, b, (((1,), (1,)), ((), ())), preferred_element_type=F32)


class Plan:
    def __init__(self, dom, rep, spline, face_dest, flow_rhs, send_list):
        self.dom, self.rep = dom, rep
        self.blocks = spline.shape[0]
        self.faces = face_dest.shape[0]
        self.own_faces = self.faces // rep
        self.pairs = flow_rhs.shape[2]
        self.comps = flow_rhs.shape[0]
        self.cells = flow_rhs.shape[3]
        self.halo = send_list.shape[1]
        self.part_rows = 2 * self.pairs
        self.rows = self.comps * self.part_rows
        self.row_pad = -(-self.rows // 8) * 8
        self.values = 2 * self.part_rows
        self.cap = 2 * self.faces // dom
        self.width = min(2 * LANES, self.cap)
        self.steps = self.cap // self.width
        count = self.values + 1
        while count * self.steps % 8:
            count += 1
        self.slot_rows = count * self.steps
        spare = self.slot_rows - (self.values + 1) * self.steps
        self.compact = self.width == 2 * LANES and spare == self.steps
        self.sent_rows = self.slot_rows * (self.width // LANES)
        if self.compact:
            self.sent_rows -= 2 * self.steps
        self.chunks = self.cells // LANES
        self.wide = min(2 * LANES, self.halo)
        self.face_chunks = self.faces // LANES


def kernel(
    pn,
    *refs,
):
    hbm, out_ref, staged, (load_sem, *refs) = refs[:12], refs[12], refs[13:25], refs[25:]
    (
        freq_ref,
        coeff_ref,
        spline_ref,
        dest_ref,
        cell_ref,
        prev_ref,
        send_ref,
        neighbor_ref,
        jac_ref,
        diag_ref,
        weight_ref,
        flow_ref,
    ) = staged
    (
        part_buf,
        face_buf,
        slot_buf,
        left_buf,
        right_buf,
        slot_sum,
        pack_buf,
        recv_buf,
        add_left,
        add_right,
        wall_buf,
        field,
        table,
        table_far,
        hot_send,
        hot_near,
        high_buf,
        near,
        ghost,
        halo_send,
        beside,
        jac,
        diag,
        weight,
        flow,
        iterate,
        coupled,
        rep_send_sem,
        rep_recv_sem,
        dom_send_sem,
        dom_recv_sem,
        halo_send_sem,
        halo_recv_sem,
    ) = refs
    loads = [pltpu.make_async_copy(hbm[i], staged[i], load_sem.at[i]) for i in range(12)]
    for load in loads:
        load.start()
    me_dom, me_rep = lax.axis_index("dom"), lax.axis_index("rep")
    n_ch, rows, rpad, width = pn.chunks, pn.rows, pn.row_pad, pn.part_rows
    groups = rpad // 8

    barrier = pltpu.get_barrier_semaphore()
    for offset in range(1, pn.rep):
        pl.semaphore_signal(
            barrier, inc=1, device_id=(me_dom, lax.rem(me_rep + offset, pn.rep)), device_id_type=MESH
        )

    def greet(offset, carry):
        pl.semaphore_signal(
            barrier, inc=1, device_id=(lax.rem(me_dom + offset, pn.dom), me_rep), device_id_type=MESH
        )
        return carry

    lax.fori_loop(1, pn.dom, greet, 0)

    row_id = iota((pn.rep * pn.values, LANES), 0)
    pair_id = row_id // pn.values * pn.pairs + row_id % pn.pairs
    scale = jnp.zeros(row_id.shape, F32)
    loads[0].wait()
    for pair in range(pn.rep * pn.pairs):
        scale = jnp.where(pair_id == pair, freq_ref[pair], scale)
    scale = jnp.where(row_id // pn.pairs % 2 == 0, -scale, scale)
    scale = jnp.where(row_id // width % 2 == 0, scale, 1.0)
    loads[1].wait()
    all_pairs = pn.rep * pn.pairs
    shape = (pn.rep * pn.values, 2 * all_pairs)
    row_id, column = iota(shape, 0), iota(shape, 1)
    part_id = row_id // pn.pairs % 2
    pair_id = row_id // pn.values * pn.pairs + row_id % pn.pairs
    coeffs = []
    for q in range(2):
        source = part_id if q == 1 else 1 - part_id
        chosen = (row_id // width % 2 == q) & (column == source * all_pairs + pair_id)
        chosen = jnp.where(chosen, 1.0, 0.0).astype(BF16)
        coeffs.append(jnp.dot(chosen, coeff_ref[...], preferred_element_type=F32).astype(BF16))
    modes = coeff_ref.shape[1]
    loads[2].wait()
    for block in range(pn.blocks):
        base = jnp.dot(coeffs[0], spline_ref[block, :modes], preferred_element_type=F32)
        base += jnp.dot(coeffs[1], spline_ref[block, modes:], preferred_element_type=F32)
        base *= scale
        for peer in range(pn.rep):
            part_buf[peer, :, block * LANES : (block + 1) * LANES] = base[
                peer * pn.values : (peer + 1) * pn.values
            ]

    pl.semaphore_wait(barrier, pn.rep - 1 + pn.dom - 1)

    def rep_copy(offset):
        peer = lax.rem(me_rep + offset, pn.rep)
        return pltpu.make_async_remote_copy(
            src_ref=part_buf.at[peer],
            dst_ref=face_buf.at[me_rep],
            send_sem=rep_send_sem.at[offset],
            recv_sem=rep_recv_sem.at[offset],
            device_id=(me_dom, peer),
            device_id_type=MESH,
        )

    for offset in range(1, pn.rep):
        rep_copy(offset).start()
    face_buf[me_rep] = part_buf[me_rep]

    group = min(8, pn.dom)
    lines = pn.face_chunks
    tri = jnp.where(
        (iota((LANES, 2 * LANES), 1) >= LANES)
        | (iota((LANES, 2 * LANES), 0) <= iota((LANES, 2 * LANES), 1)),
        1.0,
        0.0,
    ).astype(BF16)
    size = group * lines
    above = jnp.where(
        (iota((size, size), 0) // lines == iota((size, size), 1) // lines)
        & (iota((size, size), 1) < iota((size, size), 0)),
        1.0,
        0.0,
    ).astype(BF16)
    loads[3].wait()
    ahead = pn.dom // 4
    dest = remainder(dest_ref[...] - me_dom + (2 * pn.dom - ahead), pn.dom)
    slots = jnp.zeros((lines, LANES), F32)
    for first in range(0, pn.dom, group):
        mask = jnp.concatenate(
            [jnp.where(dest == first + d, 1.0, 0.0) for d in range(group)], axis=0
        )
        counts = jnp.dot(mask.astype(BF16), tri, preferred_element_type=F32)
        before = jnp.dot(above, counts[:, LANES:].astype(BF16), preferred_element_type=F32)
        place = mask * (counts[:, :LANES] + before - 1.0)
        for d in range(group):
            part = slice(d * lines, (d + 1) * lines)
            slots = slots + place[part] + mask[part] * float((first + d) * pn.cap)
    slot_buf[...] = slots.astype(jnp.int32)

    def unfold(source, target, base):
        for tile in range(n_ch):
            target[pl.ds(base + tile, source.shape[0], stride=n_ch), :] = source[
                :, tile * LANES : (tile + 1) * LANES
            ]

    wide, n_wide = pn.wide, pn.cells // pn.wide
    per_wide = wide // LANES
    n_faces = neighbor_ref.shape[0]

    def spread_field():
        for row in range(rows):
            field[pl.ds(row, n_ch, stride=rpad), :] = iterate[row * n_ch : (row + 1) * n_ch]
        blocks = [
            jnp.concatenate(
                [
                    field[chunk * rpad : (chunk + 1) * rpad, :]
                    for chunk in range(c * per_wide, (c + 1) * per_wide)
                ],
                axis=1,
            )
            for c in range(n_wide)
        ]
        table[:, :wide], table[:, wide:] = split(jnp.concatenate(blocks, axis=0))

    def pick(parts, first_chunk, count, hot, high, start):
        found = jnp.dot(parts, jnp.concatenate([hot, hot], axis=0), preferred_element_type=F32)
        picked = list(start)
        for chunk in range(count):
            here = high == first_chunk + chunk
            for g in range(groups):
                at = chunk * rpad + g * 8
                picked[g] = jnp.where(here, found[at : at + 8], picked[g])
        return picked

    def one_hot(low, target):
        both = jnp.concatenate([low, low], axis=0)

        def body(turn, carry):
            first = pl.multiple_of(turn * 16, 16)
            target[pl.ds(first, 16), :] = jnp.where(
                both == iota(both.shape, 0) + first, 1.0, 0.0
            ).astype(BF16)
            return carry

        lax.fori_loop(0, wide // 16, body, 0)

    def halo_copy(sweep, block):
        return pltpu.make_async_remote_copy(
            src_ref=halo_send.at[sweep, block],
            dst_ref=ghost.at[sweep, block],
            send_sem=halo_send_sem.at[sweep, block],
            recv_sem=halo_recv_sem.at[sweep, block],
            device_id=(lax.rem(me_dom + OFFSETS[block] + pn.dom, pn.dom), me_rep),
            device_id_type=MESH,
        )

    def send_halo(sweep):
        for block in range(4):
            index = jnp.broadcast_to(send_ref[block : block + 1, :], (8, pn.halo))
            zeros = [jnp.zeros((8, pn.halo), F32)] * groups
            found = pick(table[...], 0, n_wide, hot_send[block], quotient(index, wide), zeros)
            for g in range(groups):
                halo_send[sweep, block, g * 8 : g * 8 + 8, :] = found[g]
            halo_copy(sweep, block).start()

    def gather_local():
        def body(face, carry):
            high = high_buf[face]
            zeros = [jnp.zeros(high.shape, F32)] * groups
            found = pick(table[...], 0, n_wide, hot_near[face], high, zeros)
            for g in range(groups):
                near[face, g * 8 : g * 8 + 8, :] = found[g]
            return carry

        lax.fori_loop(0, n_faces, body, 0)

    n_ghost = pn.halo // wide

    def gather_ghost(sweep):
        for block in range(4):
            halo_copy(sweep, block).wait()
        blocks = []
        for chunk in range(4 * n_ghost):
            lane = chunk % n_ghost * wide
            blocks.append(ghost[sweep, chunk // n_ghost, :, lane : lane + wide])
        table_far[:, :wide], table_far[:, wide:] = split(jnp.concatenate(blocks, axis=0))

        def body(face, carry):
            start = [near[face, g * 8 : g * 8 + 8, :] for g in range(groups)]
            found = pick(table_far[...], n_wide, 4 * n_ghost, hot_near[face], high_buf[face], start)
            for g in range(groups):
                count = min(8, rows - g * 8)
                for tile in range(n_ch):
                    where = pl.ds((face * rows + g * 8) * n_ch + tile, count, stride=n_ch)
                    beside[where, :] = found[g][:count, tile * LANES : (tile + 1) * LANES]
            return carry

        lax.fori_loop(0, n_faces, body, 0)

    def line(ref, index):
        return ref[pl.ds(pl.multiple_of(index * n_ch, n_ch), n_ch), :]

    def couple():
        def body(e, carry):
            total = [jnp.zeros((n_ch, LANES), F32)] * width
            for face in range(n_faces):
                for g in range(pn.comps):
                    entry = line(jac, (e * pn.comps + g) * n_faces + face)
                    for k in range(width):
                        total[k] = total[k] + entry * line(beside, face * rows + g * width + k)
            for k in range(width):
                coupled[pl.ds(pl.multiple_of((e * width + k) * n_ch, n_ch), n_ch), :] = total[k]
            return carry

        lax.fori_loop(0, pn.comps, body, 0)

    def update():
        own = [freq_ref[me_rep * pn.pairs + p] for p in range(pn.pairs)]
        for k in range(width):
            part, pair = k // pn.pairs, k % pn.pairs
            turned = (1 - part) * pn.pairs + pair
            sign = own[pair] if part == 0 else -own[pair]
            residual = []
            for g in range(pn.comps):
                row = g * width + k
                residual.append(
                    line(flow, row) - line(coupled, row) + sign * line(iterate, g * width + turned)
                )
            for e in range(pn.comps):
                total = line(diag, e * pn.comps) * residual[0]
                for g in range(1, pn.comps):
                    total = total + line(diag, e * pn.comps + g) * residual[g]
                row = e * width + k
                coupled[row * n_ch : (row + 1) * n_ch, :] = total
        for row in range(rows):
            iterate[row * n_ch : (row + 1) * n_ch, :] = line(coupled, row)

    loads[4].wait()

    def low_hot(chunk, carry):
        low = remainder(slot_buf[pl.ds(chunk, 1), :], pn.width)
        low = jnp.broadcast_to(low, (pn.width, LANES))
        where = pl.ds(pl.multiple_of(chunk * LANES, LANES), LANES)
        right_buf[:, where] = jnp.where(low == iota(low.shape, 0), 1.0, 0.0).astype(BF16)
        return carry

    lax.fori_loop(0, lines, low_hot, 0)

    for offset in range(1, pn.rep):
        rep_copy(offset).wait()

    per = 8 if lines % 8 == 0 else 1
    half_dom = pn.dom // 2
    n_slot = half_dom * pn.slot_rows
    slot_half = slice(0, n_slot), slice(n_slot, 2 * n_slot)

    def pack(first_place, turn, carry):
        for c in range(per):
            chunk = turn * per + c
            lanes = slice(c * LANES, (c + 1) * LANES)
            slot = slot_buf[pl.ds(chunk, 1), :]
            owner = chunk // pn.blocks
            column = pl.multiple_of(chunk % pn.blocks * LANES, LANES)
            value = face_buf[owner, :, pl.ds(column, LANES)]
            cell = cell_ref[pl.ds(chunk, 1), :].astype(F32)
            high = jnp.broadcast_to(quotient(slot, pn.width), (8, LANES))
            sub = iota((8, LANES), 0)
            parts = []
            for tile in range(pn.slot_rows // 8):
                row = jnp.zeros((8, LANES), F32)
                for v in range(pn.values + 1):
                    source = value[v : v + 1] if v < pn.values else cell
                    low_row, top_row = v * pn.steps - tile * 8, (v + 1) * pn.steps - tile * 8
                    if top_row <= 0 or low_row >= 8:
                        continue
                    inside = (sub >= low_row) & (sub < top_row)
                    row = jnp.where(inside, jnp.broadcast_to(source, (8, LANES)), row)
                parts.append([part.astype(F32) for part in split(row)])
            halves = ([], [])
            for d in range(half_dom):
                for tile in range(pn.slot_rows // 8):
                    step = remainder(sub + tile * 8, pn.steps)
                    here = high == (first_place + d) * pn.steps + step
                    for half in range(2):
                        halves[half].append(jnp.where(here, parts[tile][half], 0.0))
            for half in range(2):
                left_buf[slot_half[half], lanes] = jnp.concatenate(halves[half], axis=0).astype(BF16)
        where = pl.ds(pl.multiple_of(turn * per * LANES, per * LANES), per * LANES)
        found = dot_last(left_buf[...], right_buf[:, where])
        slot_sum[...] += found[:n_slot] + found[n_slot:]
        return carry

    def dom_copy(place):
        target = lax.rem(me_dom + place + ahead, pn.dom)
        return pltpu.make_async_remote_copy(
            src_ref=pack_buf.at[place],
            dst_ref=recv_buf.at[place],
            send_sem=dom_send_sem.at[place],
            recv_sem=dom_recv_sem.at[place],
            device_id=(target, me_rep),
            device_id_type=MESH,
        )

    def send_faces(place, carry):
        dom_copy(place).start()
        return carry

    own_place = pn.dom - ahead
    filled = pn.values * pn.steps
    for first_place in (0, half_dom):
        slot_sum[...] = jnp.zeros(slot_sum.shape, F32)
        lax.fori_loop(0, lines // per, functools.partial(pack, first_place), 0)
        for d in range(half_dom):
            a = d * pn.slot_rows
            if pn.compact:
                found = slot_sum[a : a + pn.slot_rows, :LANES]
                other = slot_sum[a : a + pn.slot_rows, LANES:]
                pack_buf[first_place + d] = jnp.concatenate(
                    [found[: filled + pn.steps], other[filled : filled + pn.steps], other[:filled]], axis=0
                )
            else:
                for part in range(pn.width // LANES):
                    pack_buf[
                        first_place + d, part * pn.slot_rows : (part + 1) * pn.slot_rows, :
                    ] = slot_sum[a : a + pn.slot_rows, part * LANES : (part + 1) * LANES]
        if first_place == 0:
            lax.fori_loop(0, half_dom, send_faces, 0)
        else:
            lax.fori_loop(half_dom, own_place, send_faces, 0)
            lax.fori_loop(own_place + 1, pn.dom, send_faces, 0)
    recv_buf[own_place] = pack_buf[own_place]

    loads[5].wait()
    for e in range(pn.comps):
        for r in range(2):
            unfold(prev_ref[e, r], iterate, (e * width + r * pn.pairs) * n_ch)
    loads[6].wait()
    field[...] = jnp.zeros(field.shape, F32)
    spread_field()
    for block in range(4):
        index = jnp.broadcast_to(send_ref[block : block + 1, :], (8, pn.halo))
        one_hot(remainder(index, wide), hot_send.at[block])
    send_halo(0)

    for load in loads[7:]:
        load.wait()
    def unfold_jac(index, carry):
        unfold(jac_ref[index].astype(F32), jac, index * (n_faces * n_ch))
        return carry

    lax.fori_loop(0, pn.comps * pn.comps, unfold_jac, 0)
    for face in range(n_faces):
        index = jnp.broadcast_to(neighbor_ref[face : face + 1, :], (8, pn.cells))
        high_buf[face] = quotient(index, wide)
        one_hot(remainder(index, wide), hot_near.at[face])
    for e in range(pn.comps):
        unfold(diag_ref[e], diag, e * pn.comps * n_ch)
        unfold(weight_ref[e], weight, e * 2 * n_ch)
        for r in range(2):
            unfold(flow_ref[e, r], flow, (e * width + r * pn.pairs) * n_ch)
    gather_local()
    gather_ghost(0)
    couple()

    wall_buf[...] = jnp.zeros(wall_buf.shape, F32)
    half_rows = pn.values * n_ch

    def add_faces(offset):
        for step in range(pn.steps):
            for part in range(pn.width // LANES):
                place = step * pn.width + part * LANES
                if pn.compact:
                    top, cell_row = part * pn.slot_rows, filled + step + part * pn.steps
                else:
                    top, cell_row = part * pn.slot_rows, filled + step + part * pn.slot_rows
                cell = recv_buf[offset, cell_row : cell_row + 1, :].astype(jnp.int32)
                low = jnp.broadcast_to(remainder(cell, LANES), (LANES, LANES))
                add_right[:, place : place + LANES] = jnp.where(
                    low == iota((LANES, LANES), 0), 1.0, 0.0
                ).astype(BF16)
                here = jnp.broadcast_to(quotient(cell, LANES), (n_ch, LANES)) == iota((n_ch, LANES), 0)
                for v in range(pn.values):
                    row = top + v * pn.steps + step
                    value = jnp.broadcast_to(recv_buf[offset, row : row + 1, :], (n_ch, LANES))
                    first, second = split(jnp.where(here, value, 0.0))
                    add_left[v * n_ch : (v + 1) * n_ch, place : place + LANES] = first
                    add_left[
                        half_rows + v * n_ch : half_rows + (v + 1) * n_ch, place : place + LANES
                    ] = second
        found = dot_last(add_left[...], add_right[...])
        wall_buf[...] += found[:half_rows] + found[half_rows:]

    add_faces(own_place)

    def receive(offset, carry):
        dom_copy(offset).wait()
        add_faces(offset)
        return carry

    lax.fori_loop(0, own_place, receive, 0)
    lax.fori_loop(own_place + 1, pn.dom, receive, 0)

    for e in range(pn.comps):
        first, second = line(weight, 2 * e), line(weight, 2 * e + 1)
        for k in range(width):
            row = e * width + k
            flow[row * n_ch : (row + 1) * n_ch, :] = (
                line(flow, row) + first * line(wall_buf, k) + second * line(wall_buf, width + k)
            )

    update()
    for sweep in range(1, SWEEPS):
        spread_field()
        send_halo(sweep)
        gather_local()
        gather_ghost(sweep)
        couple()
        update()

    for e in range(pn.comps):
        for r in range(2):
            for tile in range(n_ch):
                start = (e * width + r * pn.pairs) * n_ch + tile
                out_ref[e, r, :, tile * LANES : (tile + 1) * LANES] = iterate[
                    pl.ds(start, pn.pairs, stride=n_ch), :
                ]


def shards(
    dom,
    rep,
    spline_blocks,
    modal_coeff,
    frequency,
    face_dest,
    face_cell,
    wall_weight,
    flow_rhs,
    previous,
    diag_inverse,
    off_jacobian,
    neighbor,
    send_list,
):
    pn = Plan(dom, rep, spline_blocks, face_dest, flow_rhs, send_list)
    modes = modal_coeff.shape[0]
    operands = (
        frequency,
        jnp.transpose(modal_coeff, (1, 2, 0)).reshape(2 * rep * pn.pairs, modes),
        spline_blocks.reshape(pn.blocks, 2 * modes, LANES),
        face_dest.reshape(pn.face_chunks, LANES),
        face_cell.reshape(pn.face_chunks, LANES),
        previous,
        send_list,
        neighbor,
        jnp.transpose(off_jacobian, (1, 2, 0, 3)).reshape(
            pn.comps * pn.comps, neighbor.shape[0], pn.cells
        ),
        diag_inverse,
        wall_weight,
        flow_rhs,
    )
    n_faces = neighbor.shape[0]
    lines = pn.face_chunks
    per = 8 if lines % 8 == 0 else 1
    vmem = pl.BlockSpec(memory_space=pltpu.VMEM)
    return pl.pallas_call(
        functools.partial(kernel, pn),
        out_shape=jax.ShapeDtypeStruct(previous.shape, F32),
        in_specs=[pl.BlockSpec(memory_space=pltpu.HBM)] * len(operands),
        out_specs=vmem,
        scratch_shapes=[pltpu.SMEM(frequency.shape, F32)]
        + [pltpu.VMEM(value.shape, value.dtype) for value in operands[1:]]
        + [
            pltpu.SemaphoreType.DMA((len(operands),)),
            pltpu.VMEM((rep, pn.values, pn.own_faces), F32),
            pltpu.VMEM((rep, pn.values, pn.own_faces), F32),
            pltpu.VMEM((lines, LANES), jnp.int32),
            pltpu.VMEM((dom * pn.slot_rows, per * LANES), BF16),
            pltpu.VMEM((pn.width, pn.faces), BF16),
            pltpu.VMEM((dom // 2 * pn.slot_rows, pn.width), F32),
            pltpu.VMEM((dom, pn.sent_rows, LANES), F32),
            pltpu.VMEM((dom, pn.sent_rows, LANES), F32),
            pltpu.VMEM((2 * pn.values * pn.chunks, pn.cap), BF16),
            pltpu.VMEM((LANES, pn.cap), BF16),
            pltpu.VMEM((pn.values * pn.chunks, LANES), F32),
            pltpu.VMEM((pn.chunks * pn.row_pad, LANES), F32),
            pltpu.VMEM((pn.cells // pn.wide * pn.row_pad, 2 * pn.wide), BF16),
            pltpu.VMEM((4 * pn.halo // pn.wide * pn.row_pad, 2 * pn.wide), BF16),
            pltpu.VMEM((4, pn.wide, pn.halo), BF16),
            pltpu.VMEM((n_faces, pn.wide, pn.cells), BF16),
            pltpu.VMEM((n_faces, 8, pn.cells), jnp.int32),
            pltpu.VMEM((n_faces, pn.row_pad, pn.cells), F32),
            pltpu.VMEM((SWEEPS, 4, pn.row_pad, pn.halo), F32),
            pltpu.VMEM((SWEEPS, 4, pn.row_pad, pn.halo), F32),
            pltpu.VMEM((n_faces * pn.rows * pn.chunks, LANES), F32),
            pltpu.VMEM((n_faces * pn.comps * pn.comps * pn.chunks, LANES), F32),
            pltpu.VMEM((pn.comps * pn.comps * pn.chunks, LANES), F32),
            pltpu.VMEM((pn.comps * 2 * pn.chunks, LANES), F32),
            pltpu.VMEM((pn.rows * pn.chunks, LANES), F32),
            pltpu.VMEM((pn.rows * pn.chunks, LANES), F32),
            pltpu.VMEM((pn.rows * pn.chunks, LANES), F32),
            pltpu.SemaphoreType.DMA((rep,)),
            pltpu.SemaphoreType.DMA((rep,)),
            pltpu.SemaphoreType.DMA((dom,)),
            pltpu.SemaphoreType.DMA((dom,)),
            pltpu.SemaphoreType.DMA((SWEEPS, 4)),
            pltpu.SemaphoreType.DMA((SWEEPS, 4)),
        ],
        compiler_params=pltpu.CompilerParams(
            collective_id=0, has_side_effects=True, vmem_limit_bytes=63 * 1024 * 1024
        ),
    )(*operands)


def solution(mesh):
    return jax.shard_map(
        functools.partial(shards, mesh.shape["dom"], mesh.shape["rep"]),
        mesh=mesh,
        in_specs=(
            P(("dom", "rep"), None, None, None),
            P(),
            P(),
            P("dom", None),
            P("dom"),
            P(None, None, "dom"),
            P(None, None, "rep", "dom"),
            P(None, None, "rep", "dom"),
            P(None, None, "dom"),
            P(None, None, None, "dom"),
            P(None, "dom"),
            P(None, "dom"),
        ),
        out_specs=P(None, None, "rep", "dom"),
        check_vma=False,
    )
```

```python
import functools

import jax
import jax.numpy as jnp
from jax import lax
from jax.experimental import pallas as pl
from jax.experimental.pallas import tpu as pltpu
from jax.sharding import PartitionSpec as P

SWEEPS = 2
OFFSETS = (1, -1, 2, -2)
LANES = 128
MESH = pl.DeviceIdType.MESH
F32 = jnp.float32
BF16 = jnp.bfloat16


def iota(shape, axis):
    return lax.broadcasted_iota(jnp.int32, shape, axis)


def remainder(value, size):
    return value & (size - 1) if size & (size - 1) == 0 else value % size


def quotient(value, size):
    return value >> (size.bit_length() - 1) if size & (size - 1) == 0 else value // size


def split(value):
    high = value.astype(BF16)
    return high, (value - high.astype(F32)).astype(BF16)


def dot_last(a, b):
    return lax.dot_general(a, b, (((1,), (1,)), ((), ())), preferred_element_type=F32)


class Plan:
    def __init__(self, dom, rep, spline, face_dest, flow_rhs, send_list):
        self.dom, self.rep = dom, rep
        self.blocks = spline.shape[0]
        self.faces = face_dest.shape[0]
        self.own_faces = self.faces // rep
        self.pairs = flow_rhs.shape[2]
        self.comps = flow_rhs.shape[0]
        self.cells = flow_rhs.shape[3]
        self.halo = send_list.shape[1]
        self.part_rows = 2 * self.pairs
        self.rows = self.comps * self.part_rows
        self.row_pad = -(-self.rows // 8) * 8
        self.values = 2 * self.part_rows
        self.cap = 2 * self.faces // dom
        self.width = min(2 * LANES, self.cap)
        self.steps = self.cap // self.width
        count = self.values + 1
        while count * self.steps % 8:
            count += 1
        self.slot_rows = count * self.steps
        spare = self.slot_rows - (self.values + 1) * self.steps
        self.compact = self.width == 2 * LANES and spare == self.steps
        self.sent_rows = self.slot_rows * (self.width // LANES)
        if self.compact:
            self.sent_rows -= 2 * self.steps
        self.chunks = self.cells // LANES
        self.wide = min(2 * LANES, self.halo)
        self.face_chunks = self.faces // LANES


def kernel(
    pn,
    *refs,
):
    hbm, out_ref, staged, (load_sem, *refs) = refs[:12], refs[12], refs[13:25], refs[25:]
    (
        freq_ref,
        coeff_ref,
        spline_ref,
        dest_ref,
        cell_ref,
        prev_ref,
        send_ref,
        neighbor_ref,
        jac_ref,
        diag_ref,
        weight_ref,
        flow_ref,
    ) = staged
    (
        part_buf,
        face_buf,
        slot_buf,
        left_buf,
        right_buf,
        slot_sum,
        pack_buf,
        recv_buf,
        add_left,
        add_right,
        wall_buf,
        field,
        table,
        hot_send,
        hot_near,
        high_buf,
        near,
        ghost,
        halo_send,
        beside,
        jac,
        diag,
        weight,
        flow,
        iterate,
        coupled,
        rep_send_sem,
        rep_recv_sem,
        dom_send_sem,
        dom_recv_sem,
        halo_send_sem,
        halo_recv_sem,
    ) = refs
    loads = [pltpu.make_async_copy(hbm[i], staged[i], load_sem.at[i]) for i in range(12)]
    for load in loads:
        load.start()
    me_dom, me_rep = lax.axis_index("dom"), lax.axis_index("rep")
    n_ch, rows, rpad, width = pn.chunks, pn.rows, pn.row_pad, pn.part_rows
    groups = rpad // 8

    barrier = pltpu.get_barrier_semaphore()
    for offset in range(1, pn.rep):
        pl.semaphore_signal(
            barrier, inc=1, device_id=(me_dom, lax.rem(me_rep + offset, pn.rep)), device_id_type=MESH
        )

    def greet(offset, carry):
        pl.semaphore_signal(
            barrier, inc=1, device_id=(lax.rem(me_dom + offset, pn.dom), me_rep), device_id_type=MESH
        )
        return carry

    lax.fori_loop(1, pn.dom, greet, 0)

    row_id = iota((pn.rep * pn.values, LANES), 0)
    pair_id = row_id // pn.values * pn.pairs + row_id % pn.pairs
    scale = jnp.zeros(row_id.shape, F32)
    loads[0].wait()
    for pair in range(pn.rep * pn.pairs):
        scale = jnp.where(pair_id == pair, freq_ref[pair], scale)
    scale = jnp.where(row_id // pn.pairs % 2 == 0, -scale, scale)
    scale = jnp.where(row_id // width % 2 == 0, scale, 1.0)
    loads[1].wait()
    all_pairs = pn.rep * pn.pairs
    shape = (pn.rep * pn.values, 2 * all_pairs)
    row_id, column = iota(shape, 0), iota(shape, 1)
    part_id = row_id // pn.pairs % 2
    pair_id = row_id // pn.values * pn.pairs + row_id % pn.pairs
    coeffs = []
    for q in range(2):
        source = part_id if q == 1 else 1 - part_id
        chosen = (row_id // width % 2 == q) & (column == source * all_pairs + pair_id)
        chosen = jnp.where(chosen, 1.0, 0.0).astype(BF16)
        coeffs.append(jnp.dot(chosen, coeff_ref[...], preferred_element_type=F32).astype(BF16))
    modes = coeff_ref.shape[1]
    loads[2].wait()
    for block in range(pn.blocks):
        base = jnp.dot(coeffs[0], spline_ref[block, :modes], preferred_element_type=F32)
        base += jnp.dot(coeffs[1], spline_ref[block, modes:], preferred_element_type=F32)
        base *= scale
        for peer in range(pn.rep):
            part_buf[peer, :, block * LANES : (block + 1) * LANES] = base[
                peer * pn.values : (peer + 1) * pn.values
            ]

    pl.semaphore_wait(barrier, pn.rep - 1 + pn.dom - 1)

    def rep_copy(offset):
        peer = lax.rem(me_rep + offset, pn.rep)
        return pltpu.make_async_remote_copy(
            src_ref=part_buf.at[peer],
            dst_ref=face_buf.at[me_rep],
            send_sem=rep_send_sem.at[offset],
            recv_sem=rep_recv_sem.at[offset],
            device_id=(me_dom, peer),
            device_id_type=MESH,
        )

    for offset in range(1, pn.rep):
        rep_copy(offset).start()
    face_buf[me_rep] = part_buf[me_rep]

    group = min(8, pn.dom)
    lines = pn.face_chunks
    tri = jnp.where(
        (iota((LANES, 2 * LANES), 1) >= LANES)
        | (iota((LANES, 2 * LANES), 0) <= iota((LANES, 2 * LANES), 1)),
        1.0,
        0.0,
    ).astype(BF16)
    size = group * lines
    above = jnp.where(
        (iota((size, size), 0) // lines == iota((size, size), 1) // lines)
        & (iota((size, size), 1) < iota((size, size), 0)),
        1.0,
        0.0,
    ).astype(BF16)
    loads[3].wait()
    ahead = pn.dom // 4
    dest = remainder(dest_ref[...] - me_dom + (2 * pn.dom - ahead), pn.dom)
    slots = jnp.zeros((lines, LANES), F32)
    for first in range(0, pn.dom, group):
        mask = jnp.concatenate(
            [jnp.where(dest == first + d, 1.0, 0.0) for d in range(group)], axis=0
        )
        counts = jnp.dot(mask.astype(BF16), tri, preferred_element_type=F32)
        before = jnp.dot(above, counts[:, LANES:].astype(BF16), preferred_element_type=F32)
        place = mask * (counts[:, :LANES] + before - 1.0)
        for d in range(group):
            part = slice(d * lines, (d + 1) * lines)
            slots = slots + place[part] + mask[part] * float((first + d) * pn.cap)
    slot_buf[...] = slots.astype(jnp.int32)

    def unfold(source, target, base):
        for tile in range(n_ch):
            target[pl.ds(base + tile, source.shape[0], stride=n_ch), :] = source[
                :, tile * LANES : (tile + 1) * LANES
            ]

    wide, n_wide = pn.wide, pn.cells // pn.wide
    per_wide = wide // LANES
    n_faces = neighbor_ref.shape[0]

    n_full = rows // 8
    sub = iota((8, wide), 0)

    def spread_field():
        for row in range(rows):
            value = iterate[row * n_ch : (row + 1) * n_ch]
            field[pl.ds(row, n_ch, stride=rpad), :] = value
            if row >= n_full * 8:
                field[pl.ds(row + 4, n_ch, stride=rpad), :] = value
        blocks = [
            jnp.concatenate(
                [
                    field[chunk * rpad : (chunk + 1) * rpad, :]
                    for chunk in range(c * per_wide, (c + 1) * per_wide)
                ],
                axis=1,
            )
            for c in range(n_wide)
        ]
        fill_table(blocks, 0)

    def fill_table(blocks, first):
        count = len(blocks)
        tiles = [block[g * 8 : g * 8 + 8] for g in range(n_full) for block in blocks]
        for c in range(count // 2):
            a, b = blocks[c][n_full * 8 :], blocks[c + count // 2][n_full * 8 :]
            tiles.append(jnp.where(sub < 4, a, b))
        where = slice(first, first + len(tiles) * 8)
        table[where, :wide], table[where, wide:] = split(jnp.concatenate(tiles, axis=0))

    def table_rows(count):
        return (n_full * count + count // 2) * 8

    near_rows, far_rows = table_rows(n_wide), table_rows(4 * pn.halo // wide)

    def multiply(first, count, hot):
        return jnp.dot(
            table[first : first + count, :],
            jnp.concatenate([hot, hot], axis=0),
            preferred_element_type=F32,
        )

    def choose(found, first_chunk, count, high, start):
        picked = list(start)
        late = jnp.where(iota(high.shape, 0) < 4, high, high - count // 2)
        for chunk in range(count):
            here = high == first_chunk + chunk
            for g in range(n_full):
                at = (g * count + chunk) * 8
                picked[g] = jnp.where(here, found[at : at + 8], picked[g])
        for chunk in range(count // 2):
            at = (n_full * count + chunk) * 8
            picked[n_full] = jnp.where(
                late == first_chunk + chunk, found[at : at + 8], picked[n_full]
            )
        return picked

    def joined(picked):
        return picked[:n_full] + [picked[n_full] + pltpu.roll(picked[n_full], 4, axis=0)]

    def one_hot(low, target):
        both = jnp.concatenate([low, low], axis=0)

        def body(turn, carry):
            for part in range(4):
                first = pl.multiple_of(turn * 64 + part * 16, 16)
                target[pl.ds(first, 16), :] = jnp.where(
                    both == iota(both.shape, 0) + first, 1.0, 0.0
                ).astype(BF16)
            return carry

        lax.fori_loop(0, wide // 64, body, 0)

    def halo_copy(sweep, block):
        return pltpu.make_async_remote_copy(
            src_ref=halo_send.at[sweep, block],
            dst_ref=ghost.at[sweep, block],
            send_sem=halo_send_sem.at[sweep, block],
            recv_sem=halo_recv_sem.at[sweep, block],
            device_id=(lax.rem(me_dom + OFFSETS[block] + pn.dom, pn.dom), me_rep),
            device_id_type=MESH,
        )

    def send_index():
        return jnp.concatenate(
            [jnp.broadcast_to(send_ref[k : k + 1, :], (8, pn.halo)) for k in range(4)], axis=1
        )

    def send_halo(sweep):
        high = quotient(send_index(), wide)
        zeros = [jnp.zeros(high.shape, F32)] * groups
        found = joined(choose(multiply(0, near_rows, hot_send[...]), 0, n_wide, high, zeros))
        for block in range(4):
            for g in range(groups):
                halo_send[sweep, block, g * 8 : g * 8 + 8, :] = found[g][
                    :, block * pn.halo : (block + 1) * pn.halo
                ]
            halo_copy(sweep, block).start()

    n_ghost = pn.halo // wide

    def take_ghost(sweep):
        for block in range(4):
            halo_copy(sweep, block).wait()
        blocks = []
        for chunk in range(4 * n_ghost):
            lane = chunk % n_ghost * wide
            blocks.append(ghost[sweep, chunk // n_ghost, :, lane : lane + wide])
        fill_table(blocks, near_rows)

    def keep_beside(face, picked):
        found = joined(picked)
        for g in range(groups):
            count = min(8, rows - g * 8)
            for tile in range(n_ch):
                where = pl.ds((face * rows + g * 8) * n_ch + tile, count, stride=n_ch)
                beside[where, :] = found[g][:count, tile * LANES : (tile + 1) * LANES]

    def gather_local():
        def body(face, carry):
            high = high_buf[face]
            zeros = [jnp.zeros(high.shape, F32)] * groups
            found = choose(multiply(0, near_rows, hot_near[face]), 0, n_wide, high, zeros)
            for g in range(groups):
                near[face, g * 8 : g * 8 + 8, :] = found[g]
            return carry

        lax.fori_loop(0, n_faces, body, 0)

    def gather_ghost():
        def body(face, carry):
            start = [near[face, g * 8 : g * 8 + 8, :] for g in range(groups)]
            found = multiply(near_rows, far_rows, hot_near[face])
            keep_beside(face, choose(found, n_wide, 4 * n_ghost, high_buf[face], start))
            return carry

        lax.fori_loop(0, n_faces, body, 0)

    def gather_all():
        def body(face, carry):
            high = high_buf[face]
            zeros = [jnp.zeros(high.shape, F32)] * groups
            found = multiply(0, near_rows + far_rows, hot_near[face])
            some = choose(found[:near_rows], 0, n_wide, high, zeros)
            keep_beside(face, choose(found[near_rows:], n_wide, 4 * n_ghost, high, some))
            return carry

        lax.fori_loop(0, n_faces, body, 0)

    def line(ref, index):
        return ref[pl.ds(pl.multiple_of(index * n_ch, n_ch), n_ch), :]

    def couple():
        def body(e, carry):
            total = [jnp.zeros((n_ch, LANES), F32)] * width
            for face in range(n_faces):
                for g in range(pn.comps):
                    entry = line(jac, (e * pn.comps + g) * n_faces + face)
                    for k in range(width):
                        total[k] = total[k] + entry * line(beside, face * rows + g * width + k)
            for k in range(width):
                coupled[pl.ds(pl.multiple_of((e * width + k) * n_ch, n_ch), n_ch), :] = total[k]
            return carry

        lax.fori_loop(0, pn.comps, body, 0)

    def update():
        own = [freq_ref[me_rep * pn.pairs + p] for p in range(pn.pairs)]
        for k in range(width):
            part, pair = k // pn.pairs, k % pn.pairs
            turned = (1 - part) * pn.pairs + pair
            sign = own[pair] if part == 0 else -own[pair]
            residual = []
            for g in range(pn.comps):
                row = g * width + k
                residual.append(
                    line(flow, row) - line(coupled, row) + sign * line(iterate, g * width + turned)
                )
            for e in range(pn.comps):
                total = line(diag, e * pn.comps) * residual[0]
                for g in range(1, pn.comps):
                    total = total + line(diag, e * pn.comps + g) * residual[g]
                row = e * width + k
                coupled[row * n_ch : (row + 1) * n_ch, :] = total
        for row in range(rows):
            iterate[row * n_ch : (row + 1) * n_ch, :] = line(coupled, row)

    loads[4].wait()

    per = 4 if lines % 4 == 0 else 1

    def low_hot(turn, carry):
        for c in range(per):
            chunk = turn * per + c
            low = remainder(slot_buf[pl.ds(chunk, 1), :], pn.width)
            low = jnp.broadcast_to(low, (pn.width, LANES))
            where = pl.ds(pl.multiple_of(chunk * LANES, LANES), LANES)
            right_buf[:, where] = jnp.where(low == iota(low.shape, 0), 1.0, 0.0).astype(BF16)
        return carry

    lax.fori_loop(0, lines // per, low_hot, 0)

    for offset in range(1, pn.rep):
        rep_copy(offset).wait()

    half_dom = pn.dom // 2
    n_slot = half_dom * pn.slot_rows
    slot_half = slice(0, n_slot), slice(n_slot, 2 * n_slot)

    def pack(first_place, turn, carry):
        for c in range(per):
            chunk = turn * per + c
            lanes = pl.ds(pl.multiple_of(chunk * LANES, LANES), LANES)
            slot = slot_buf[pl.ds(chunk, 1), :]
            owner = chunk // pn.blocks
            column = pl.multiple_of(chunk % pn.blocks * LANES, LANES)
            value = face_buf[owner, :, pl.ds(column, LANES)]
            cell = cell_ref[pl.ds(chunk, 1), :].astype(F32)
            high = jnp.broadcast_to(quotient(slot, pn.width), (8, LANES))
            sub = iota((8, LANES), 0)
            parts = []
            for tile in range(pn.slot_rows // 8):
                row = jnp.zeros((8, LANES), F32)
                for v in range(pn.values + 1):
                    source = value[v : v + 1] if v < pn.values else cell
                    low_row, top_row = v * pn.steps - tile * 8, (v + 1) * pn.steps - tile * 8
                    if top_row <= 0 or low_row >= 8:
                        continue
                    inside = (sub >= low_row) & (sub < top_row)
                    row = jnp.where(inside, jnp.broadcast_to(source, (8, LANES)), row)
                parts.append([part.astype(F32) for part in split(row)])
            halves = ([], [])
            for d in range(half_dom):
                for tile in range(pn.slot_rows // 8):
                    step = remainder(sub + tile * 8, pn.steps)
                    here = high == (first_place + d) * pn.steps + step
                    for half in range(2):
                        halves[half].append(jnp.where(here, parts[tile][half], 0.0))
            for half in range(2):
                left_buf[slot_half[half], lanes] = jnp.concatenate(halves[half], axis=0).astype(BF16)
        return carry

    def dom_copy(place):
        target = lax.rem(me_dom + place + ahead, pn.dom)
        return pltpu.make_async_remote_copy(
            src_ref=pack_buf.at[place],
            dst_ref=recv_buf.at[place],
            send_sem=dom_send_sem.at[place],
            recv_sem=dom_recv_sem.at[place],
            device_id=(target, me_rep),
            device_id_type=MESH,
        )

    def send_faces(place, carry):
        dom_copy(place).start()
        return carry

    own_place = pn.dom - ahead
    filled = pn.values * pn.steps
    for first_place in (0, half_dom):
        lax.fori_loop(0, lines // per, functools.partial(pack, first_place), 0)
        found = dot_last(left_buf[...], right_buf[...])
        slot_sum[...] = found[:n_slot] + found[n_slot:]
        for d in range(half_dom):
            a = d * pn.slot_rows
            if pn.compact:
                found = slot_sum[a : a + pn.slot_rows, :LANES]
                other = slot_sum[a : a + pn.slot_rows, LANES:]
                pack_buf[first_place + d] = jnp.concatenate(
                    [found[: filled + pn.steps], other[filled : filled + pn.steps], other[:filled]], axis=0
                )
            else:
                for part in range(pn.width // LANES):
                    pack_buf[
                        first_place + d, part * pn.slot_rows : (part + 1) * pn.slot_rows, :
                    ] = slot_sum[a : a + pn.slot_rows, part * LANES : (part + 1) * LANES]
        if first_place == 0:
            lax.fori_loop(0, half_dom, send_faces, 0)
        else:
            lax.fori_loop(half_dom, own_place, send_faces, 0)
            lax.fori_loop(own_place + 1, pn.dom, send_faces, 0)
    recv_buf[own_place] = pack_buf[own_place]

    loads[5].wait()
    for e in range(pn.comps):
        for r in range(2):
            unfold(prev_ref[e, r], iterate, (e * width + r * pn.pairs) * n_ch)
    loads[6].wait()
    field[...] = jnp.zeros(field.shape, F32)
    spread_field()
    one_hot(remainder(send_index(), wide), hot_send)
    send_halo(0)

    for load in loads[7:]:
        load.wait()
    def unfold_jac(index, carry):
        unfold(jac_ref[index].astype(F32), jac, index * (n_faces * n_ch))
        return carry

    lax.fori_loop(0, pn.comps * pn.comps, unfold_jac, 0)
    for face in range(n_faces):
        index = jnp.broadcast_to(neighbor_ref[face : face + 1, :], (8, pn.cells))
        high_buf[face] = quotient(index, wide)
        one_hot(remainder(index, wide), hot_near.at[face])
    for e in range(pn.comps):
        unfold(diag_ref[e], diag, e * pn.comps * n_ch)
        unfold(weight_ref[e], weight, e * 2 * n_ch)
        for r in range(2):
            unfold(flow_ref[e, r], flow, (e * width + r * pn.pairs) * n_ch)
    take_ghost(0)
    gather_all()
    couple()

    half_rows = pn.values * n_ch

    def add_faces(offset):
        for step in range(pn.steps):
            for part in range(pn.width // LANES):
                place = offset * pn.cap + step * pn.width + part * LANES
                where = pl.ds(pl.multiple_of(place, LANES), LANES)
                if pn.compact:
                    top, cell_row = part * pn.slot_rows, filled + step + part * pn.steps
                else:
                    top, cell_row = part * pn.slot_rows, filled + step + part * pn.slot_rows
                cell = recv_buf[offset, cell_row : cell_row + 1, :].astype(jnp.int32)
                low = jnp.broadcast_to(remainder(cell, LANES), (LANES, LANES))
                add_right[:, where] = jnp.where(
                    low == iota((LANES, LANES), 0), 1.0, 0.0
                ).astype(BF16)
                here = jnp.broadcast_to(quotient(cell, LANES), (n_ch, LANES)) == iota((n_ch, LANES), 0)
                for v in range(pn.values):
                    row = top + v * pn.steps + step
                    value = jnp.broadcast_to(recv_buf[offset, row : row + 1, :], (n_ch, LANES))
                    first, second = split(jnp.where(here, value, 0.0))
                    add_left[v * n_ch : (v + 1) * n_ch, where] = first
                    add_left[half_rows + v * n_ch : half_rows + (v + 1) * n_ch, where] = second

    add_faces(own_place)

    def receive(offset, carry):
        dom_copy(offset).wait()
        add_faces(offset)
        return carry

    lax.fori_loop(0, own_place, receive, 0)
    lax.fori_loop(own_place + 1, pn.dom, receive, 0)
    found = dot_last(add_left[...], add_right[...])
    wall_buf[...] = found[:half_rows] + found[half_rows:]

    for e in range(pn.comps):
        first, second = line(weight, 2 * e), line(weight, 2 * e + 1)
        for k in range(width):
            row = e * width + k
            flow[row * n_ch : (row + 1) * n_ch, :] = (
                line(flow, row) + first * line(wall_buf, k) + second * line(wall_buf, width + k)
            )

    update()
    for sweep in range(1, SWEEPS):
        spread_field()
        send_halo(sweep)
        gather_local()
        take_ghost(sweep)
        gather_ghost()
        couple()
        update()

    for e in range(pn.comps):
        for r in range(2):
            for tile in range(n_ch):
                start = (e * width + r * pn.pairs) * n_ch + tile
                out_ref[e, r, :, tile * LANES : (tile + 1) * LANES] = iterate[
                    pl.ds(start, pn.pairs, stride=n_ch), :
                ]


def shards(
    dom,
    rep,
    spline_blocks,
    modal_coeff,
    frequency,
    face_dest,
    face_cell,
    wall_weight,
    flow_rhs,
    previous,
    diag_inverse,
    off_jacobian,
    neighbor,
    send_list,
):
    pn = Plan(dom, rep, spline_blocks, face_dest, flow_rhs, send_list)
    modes = modal_coeff.shape[0]
    operands = (
        frequency,
        jnp.transpose(modal_coeff, (1, 2, 0)).reshape(2 * rep * pn.pairs, modes),
        spline_blocks.reshape(pn.blocks, 2 * modes, LANES),
        face_dest.reshape(pn.face_chunks, LANES),
        face_cell.reshape(pn.face_chunks, LANES),
        previous,
        send_list,
        neighbor,
        jnp.transpose(off_jacobian, (1, 2, 0, 3)).reshape(
            pn.comps * pn.comps, neighbor.shape[0], pn.cells
        ),
        diag_inverse,
        wall_weight,
        flow_rhs,
    )
    n_faces = neighbor.shape[0]
    lines = pn.face_chunks
    vmem = pl.BlockSpec(memory_space=pltpu.VMEM)
    return pl.pallas_call(
        functools.partial(kernel, pn),
        out_shape=jax.ShapeDtypeStruct(previous.shape, F32),
        in_specs=[pl.BlockSpec(memory_space=pltpu.HBM)] * len(operands),
        out_specs=vmem,
        scratch_shapes=[pltpu.SMEM(frequency.shape, F32)]
        + [pltpu.VMEM(value.shape, value.dtype) for value in operands[1:]]
        + [
            pltpu.SemaphoreType.DMA((len(operands),)),
            pltpu.VMEM((rep, pn.values, pn.own_faces), F32),
            pltpu.VMEM((rep, pn.values, pn.own_faces), F32),
            pltpu.VMEM((lines, LANES), jnp.int32),
            pltpu.VMEM((dom * pn.slot_rows, pn.faces), BF16),
            pltpu.VMEM((pn.width, pn.faces), BF16),
            pltpu.VMEM((dom // 2 * pn.slot_rows, pn.width), F32),
            pltpu.VMEM((dom, pn.sent_rows, LANES), F32),
            pltpu.VMEM((dom, pn.sent_rows, LANES), F32),
            pltpu.VMEM((2 * pn.values * pn.chunks, dom * pn.cap), BF16),
            pltpu.VMEM((LANES, dom * pn.cap), BF16),
            pltpu.VMEM((pn.values * pn.chunks, LANES), F32),
            pltpu.VMEM((pn.chunks * pn.row_pad, LANES), F32),
            pltpu.VMEM(((pn.cells + 4 * pn.halo) // pn.wide * pn.rows, 2 * pn.wide), BF16),
            pltpu.VMEM((pn.wide, 4 * pn.halo), BF16),
            pltpu.VMEM((n_faces, pn.wide, pn.cells), BF16),
            pltpu.VMEM((n_faces, 8, pn.cells), jnp.int32),
            pltpu.VMEM((n_faces, pn.row_pad, pn.cells), F32),
            pltpu.VMEM((SWEEPS, 4, pn.row_pad, pn.halo), F32),
            pltpu.VMEM((SWEEPS, 4, pn.row_pad, pn.halo), F32),
            pltpu.VMEM((n_faces * pn.rows * pn.chunks, LANES), F32),
            pltpu.VMEM((n_faces * pn.comps * pn.comps * pn.chunks, LANES), F32),
            pltpu.VMEM((pn.comps * pn.comps * pn.chunks, LANES), F32),
            pltpu.VMEM((pn.comps * 2 * pn.chunks, LANES), F32),
            pltpu.VMEM((pn.rows * pn.chunks, LANES), F32),
            pltpu.VMEM((pn.rows * pn.chunks, LANES), F32),
            pltpu.VMEM((pn.rows * pn.chunks, LANES), F32),
            pltpu.SemaphoreType.DMA((rep,)),
            pltpu.SemaphoreType.DMA((rep,)),
            pltpu.SemaphoreType.DMA((dom,)),
            pltpu.SemaphoreType.DMA((dom,)),
            pltpu.SemaphoreType.DMA((SWEEPS, 4)),
            pltpu.SemaphoreType.DMA((SWEEPS, 4)),
        ],
        compiler_params=pltpu.CompilerParams(
            collective_id=0, has_side_effects=True, vmem_limit_bytes=63 * 1024 * 1024
        ),
    )(*operands)


def solution(mesh):
    return jax.shard_map(
        functools.partial(shards, mesh.shape["dom"], mesh.shape["rep"]),
        mesh=mesh,
        in_specs=(
            P(("dom", "rep"), None, None, None),
            P(),
            P(),
            P("dom", None),
            P("dom"),
            P(None, None, "dom"),
            P(None, None, "rep", "dom"),
            P(None, None, "rep", "dom"),
            P(None, None, "dom"),
            P(None, None, None, "dom"),
            P(None, "dom"),
            P(None, "dom"),
        ),
        out_specs=P(None, None, "rep", "dom"),
        check_vma=False,
    )
```

```python
import functools

import jax
import jax.numpy as jnp
from jax import lax
from jax.experimental import pallas as pl
from jax.experimental.pallas import tpu as pltpu
from jax.sharding import PartitionSpec as P

SWEEPS = 2
OFFSETS = (1, -1, 2, -2)
LANES = 128
MESH = pl.DeviceIdType.MESH
F32 = jnp.float32
BF16 = jnp.bfloat16


def iota(shape, axis):
    return lax.broadcasted_iota(jnp.int32, shape, axis)


def remainder(value, size):
    return value & (size - 1) if size & (size - 1) == 0 else value % size


def quotient(value, size):
    return value >> (size.bit_length() - 1) if size & (size - 1) == 0 else value // size


def split(value):
    high = value.astype(BF16)
    return high, (value - high.astype(F32)).astype(BF16)


def dot_last(a, b):
    return lax.dot_general(a, b, (((1,), (1,)), ((), ())), preferred_element_type=F32)


class Plan:
    def __init__(self, dom, rep, spline, face_dest, flow_rhs, send_list):
        self.dom, self.rep = dom, rep
        self.blocks = spline.shape[0]
        self.faces = face_dest.shape[0]
        self.own_faces = self.faces // rep
        self.pairs = flow_rhs.shape[2]
        self.comps = flow_rhs.shape[0]
        self.cells = flow_rhs.shape[3]
        self.halo = send_list.shape[1]
        self.part_rows = 2 * self.pairs
        self.rows = self.comps * self.part_rows
        self.row_pad = -(-self.rows // 8) * 8
        self.values = 2 * self.part_rows
        self.cap = 2 * self.faces // dom
        self.width = min(2 * LANES, self.cap)
        self.steps = self.cap // self.width
        count = self.values + 1
        while count * self.steps % 8:
            count += 1
        self.slot_rows = count * self.steps
        spare = self.slot_rows - (self.values + 1) * self.steps
        self.compact = self.width == 2 * LANES and spare == self.steps
        self.sent_rows = self.slot_rows * (self.width // LANES)
        if self.compact:
            self.sent_rows -= 2 * self.steps
        self.chunks = self.cells // LANES
        self.wide = min(2 * LANES, self.halo)
        self.face_chunks = self.faces // LANES


def kernel(
    pn,
    *refs,
):
    hbm, out_ref, staged, (load_sem, *refs) = refs[:12], refs[12], refs[13:25], refs[25:]
    (
        freq_ref,
        coeff_ref,
        spline_ref,
        dest_ref,
        cell_ref,
        prev_ref,
        send_ref,
        neighbor_ref,
        jac_ref,
        diag_ref,
        weight_ref,
        flow_ref,
    ) = staged
    (
        part_buf,
        face_buf,
        slot_buf,
        left_buf,
        right_buf,
        slot_sum,
        pack_buf,
        recv_buf,
        add_left,
        add_right,
        wall_buf,
        field,
        table,
        hot_send,
        hot_near,
        high_buf,
        near,
        ghost,
        halo_send,
        beside,
        jac,
        diag,
        weight,
        flow,
        iterate,
        coupled,
        rep_send_sem,
        rep_recv_sem,
        dom_send_sem,
        dom_recv_sem,
        halo_send_sem,
        halo_recv_sem,
    ) = refs
    loads = [pltpu.make_async_copy(hbm[i], staged[i], load_sem.at[i]) for i in range(12)]
    for load in loads:
        load.start()
    me_dom, me_rep = lax.axis_index("dom"), lax.axis_index("rep")
    n_ch, rows, rpad, width = pn.chunks, pn.rows, pn.row_pad, pn.part_rows
    groups = rpad // 8

    barrier = pltpu.get_barrier_semaphore()
    for offset in range(1, pn.rep):
        pl.semaphore_signal(
            barrier, inc=1, device_id=(me_dom, lax.rem(me_rep + offset, pn.rep)), device_id_type=MESH
        )

    def greet(offset, carry):
        pl.semaphore_signal(
            barrier, inc=1, device_id=(lax.rem(me_dom + offset, pn.dom), me_rep), device_id_type=MESH
        )
        return carry

    lax.fori_loop(1, pn.dom, greet, 0)

    row_id = iota((pn.rep * pn.values, LANES), 0)
    pair_id = row_id // pn.values * pn.pairs + row_id % pn.pairs
    scale = jnp.zeros(row_id.shape, F32)
    loads[0].wait()
    for pair in range(pn.rep * pn.pairs):
        scale = jnp.where(pair_id == pair, freq_ref[pair], scale)
    scale = jnp.where(row_id // pn.pairs % 2 == 0, -scale, scale)
    scale = jnp.where(row_id // width % 2 == 0, scale, 1.0)
    loads[1].wait()
    all_pairs = pn.rep * pn.pairs
    shape = (pn.rep * pn.values, 2 * all_pairs)
    row_id, column = iota(shape, 0), iota(shape, 1)
    part_id = row_id // pn.pairs % 2
    pair_id = row_id // pn.values * pn.pairs + row_id % pn.pairs
    coeffs = []
    for q in range(2):
        source = part_id if q == 1 else 1 - part_id
        chosen = (row_id // width % 2 == q) & (column == source * all_pairs + pair_id)
        chosen = jnp.where(chosen, 1.0, 0.0).astype(BF16)
        coeffs.append(jnp.dot(chosen, coeff_ref[...], preferred_element_type=F32).astype(BF16))
    modes = coeff_ref.shape[1]
    loads[2].wait()
    for block in range(pn.blocks):
        base = jnp.dot(coeffs[0], spline_ref[block, :modes], preferred_element_type=F32)
        base += jnp.dot(coeffs[1], spline_ref[block, modes:], preferred_element_type=F32)
        base *= scale
        for peer in range(pn.rep):
            part_buf[peer, :, block * LANES : (block + 1) * LANES] = base[
                peer * pn.values : (peer + 1) * pn.values
            ]

    pl.semaphore_wait(barrier, pn.rep - 1 + pn.dom - 1)

    def rep_copy(offset):
        peer = lax.rem(me_rep + offset, pn.rep)
        return pltpu.make_async_remote_copy(
            src_ref=part_buf.at[peer],
            dst_ref=face_buf.at[me_rep],
            send_sem=rep_send_sem.at[offset],
            recv_sem=rep_recv_sem.at[offset],
            device_id=(me_dom, peer),
            device_id_type=MESH,
        )

    for offset in range(1, pn.rep):
        rep_copy(offset).start()
    face_buf[me_rep] = part_buf[me_rep]

    group = min(8, pn.dom)
    lines = pn.face_chunks
    tri = jnp.where(
        (iota((LANES, 2 * LANES), 1) >= LANES)
        | (iota((LANES, 2 * LANES), 0) <= iota((LANES, 2 * LANES), 1)),
        1.0,
        0.0,
    ).astype(BF16)
    size = group * lines
    above = jnp.where(
        (iota((size, size), 0) // lines == iota((size, size), 1) // lines)
        & (iota((size, size), 1) < iota((size, size), 0)),
        1.0,
        0.0,
    ).astype(BF16)
    loads[3].wait()
    ahead = pn.dom // 4
    dest = remainder(dest_ref[...] - me_dom + (2 * pn.dom - ahead), pn.dom)
    slots = jnp.zeros((lines, LANES), F32)
    for first in range(0, pn.dom, group):
        mask = jnp.concatenate(
            [jnp.where(dest == first + d, 1.0, 0.0) for d in range(group)], axis=0
        )
        counts = jnp.dot(mask.astype(BF16), tri, preferred_element_type=F32)
        before = jnp.dot(above, counts[:, LANES:].astype(BF16), preferred_element_type=F32)
        place = mask * (counts[:, :LANES] + before - 1.0)
        for d in range(group):
            part = slice(d * lines, (d + 1) * lines)
            slots = slots + place[part] + mask[part] * float((first + d) * pn.cap)
    slot_buf[...] = slots.astype(jnp.int32)

    def unfold(source, target, base):
        for tile in range(n_ch):
            target[pl.ds(base + tile, source.shape[0], stride=n_ch), :] = source[
                :, tile * LANES : (tile + 1) * LANES
            ]

    wide, n_wide = pn.wide, pn.cells // pn.wide
    per_wide = wide // LANES
    n_faces = neighbor_ref.shape[0]

    n_full = rows // 8
    sub = iota((8, wide), 0)

    def spread_field():
        for row in range(rows):
            value = iterate[row * n_ch : (row + 1) * n_ch]
            field[pl.ds(row, n_ch, stride=rpad), :] = value
            if row >= n_full * 8:
                field[pl.ds(row + 4, n_ch, stride=rpad), :] = value
        blocks = [
            jnp.concatenate(
                [
                    field[chunk * rpad : (chunk + 1) * rpad, :]
                    for chunk in range(c * per_wide, (c + 1) * per_wide)
                ],
                axis=1,
            )
            for c in range(n_wide)
        ]
        fill_table(blocks, 0)

    def fill_table(blocks, first):
        count = len(blocks)
        tiles = [block[g * 8 : g * 8 + 8] for g in range(n_full) for block in blocks]
        for c in range(count // 2):
            a, b = blocks[c][n_full * 8 :], blocks[c + count // 2][n_full * 8 :]
            tiles.append(jnp.where(sub < 4, a, b))
        where = slice(first, first + len(tiles) * 8)
        table[where, :wide], table[where, wide:] = split(jnp.concatenate(tiles, axis=0))

    def table_rows(count):
        return (n_full * count + count // 2) * 8

    near_rows, far_rows = table_rows(n_wide), table_rows(4 * pn.halo // wide)

    def multiply(first, count, hot):
        return jnp.dot(
            table[first : first + count, :],
            jnp.concatenate([hot, hot], axis=0),
            preferred_element_type=F32,
        )

    def choose(found, first_chunk, count, high, start):
        picked = list(start)
        late = jnp.where(iota(high.shape, 0) < 4, high, high - count // 2)
        for chunk in range(count):
            here = high == first_chunk + chunk
            for g in range(n_full):
                at = (g * count + chunk) * 8
                picked[g] = jnp.where(here, found[at : at + 8], picked[g])
        for chunk in range(count // 2):
            at = (n_full * count + chunk) * 8
            picked[n_full] = jnp.where(
                late == first_chunk + chunk, found[at : at + 8], picked[n_full]
            )
        return picked

    def joined(picked):
        return picked[:n_full] + [picked[n_full] + pltpu.roll(picked[n_full], 4, axis=0)]

    def one_hot(low, target):
        both = jnp.concatenate([low, low], axis=0)

        def body(turn, carry):
            for part in range(4):
                first = pl.multiple_of(turn * 64 + part * 16, 16)
                target[pl.ds(first, 16), :] = jnp.where(
                    both == iota(both.shape, 0) + first, 1.0, 0.0
                ).astype(BF16)
            return carry

        lax.fori_loop(0, wide // 64, body, 0)

    def halo_copy(sweep, block):
        return pltpu.make_async_remote_copy(
            src_ref=halo_send.at[sweep, block],
            dst_ref=ghost.at[sweep, block],
            send_sem=halo_send_sem.at[sweep, block],
            recv_sem=halo_recv_sem.at[sweep, block],
            device_id=(lax.rem(me_dom + OFFSETS[block] + pn.dom, pn.dom), me_rep),
            device_id_type=MESH,
        )

    def send_index():
        return jnp.concatenate(
            [jnp.broadcast_to(send_ref[k : k + 1, :], (8, pn.halo)) for k in range(4)], axis=1
        )

    def send_halo(sweep):
        high = quotient(send_index(), wide)
        zeros = [jnp.zeros(high.shape, F32)] * groups
        found = joined(choose(multiply(0, near_rows, hot_send[...]), 0, n_wide, high, zeros))
        for block in range(4):
            for g in range(groups):
                halo_send[sweep, block, g * 8 : g * 8 + 8, :] = found[g][
                    :, block * pn.halo : (block + 1) * pn.halo
                ]
            halo_copy(sweep, block).start()

    n_ghost = pn.halo // wide

    def take_ghost(sweep):
        for block in range(4):
            halo_copy(sweep, block).wait()
        blocks = []
        for chunk in range(4 * n_ghost):
            lane = chunk % n_ghost * wide
            blocks.append(ghost[sweep, chunk // n_ghost, :, lane : lane + wide])
        fill_table(blocks, near_rows)

    def keep_beside(face, picked):
        found = joined(picked)
        for g in range(groups):
            count = min(8, rows - g * 8)
            for tile in range(n_ch):
                where = pl.ds((face * rows + g * 8) * n_ch + tile, count, stride=n_ch)
                beside[where, :] = found[g][:count, tile * LANES : (tile + 1) * LANES]

    def gather_local():
        def body(face, carry):
            high = high_buf[face]
            zeros = [jnp.zeros(high.shape, F32)] * groups
            found = choose(multiply(0, near_rows, hot_near[face]), 0, n_wide, high, zeros)
            for g in range(groups):
                near[face, g * 8 : g * 8 + 8, :] = found[g]
            return carry

        lax.fori_loop(0, n_faces, body, 0)

    def gather_ghost():
        def body(face, carry):
            start = [near[face, g * 8 : g * 8 + 8, :] for g in range(groups)]
            found = multiply(near_rows, far_rows, hot_near[face])
            keep_beside(face, choose(found, n_wide, 4 * n_ghost, high_buf[face], start))
            return carry

        lax.fori_loop(0, n_faces, body, 0)

    def gather_all():
        def body(face, carry):
            high = high_buf[face]
            zeros = [jnp.zeros(high.shape, F32)] * groups
            found = multiply(0, near_rows + far_rows, hot_near[face])
            some = choose(found[:near_rows], 0, n_wide, high, zeros)
            keep_beside(face, choose(found[near_rows:], n_wide, 4 * n_ghost, high, some))
            return carry

        lax.fori_loop(0, n_faces, body, 0)

    def line(ref, index):
        return ref[pl.ds(pl.multiple_of(index * n_ch, n_ch), n_ch), :]

    def couple():
        def body(e, carry):
            total = [jnp.zeros((n_ch, LANES), F32)] * width
            for face in range(n_faces):
                for g in range(pn.comps):
                    entry = line(jac, (e * pn.comps + g) * n_faces + face)
                    for k in range(width):
                        total[k] = total[k] + entry * line(beside, face * rows + g * width + k)
            for k in range(width):
                coupled[pl.ds(pl.multiple_of((e * width + k) * n_ch, n_ch), n_ch), :] = total[k]
            return carry

        lax.fori_loop(0, pn.comps, body, 0)

    def update():
        own = [freq_ref[me_rep * pn.pairs + p] for p in range(pn.pairs)]
        for k in range(width):
            part, pair = k // pn.pairs, k % pn.pairs
            turned = (1 - part) * pn.pairs + pair
            sign = own[pair] if part == 0 else -own[pair]
            residual = []
            for g in range(pn.comps):
                row = g * width + k
                residual.append(
                    line(flow, row) - line(coupled, row) + sign * line(iterate, g * width + turned)
                )
            for e in range(pn.comps):
                total = line(diag, e * pn.comps) * residual[0]
                for g in range(1, pn.comps):
                    total = total + line(diag, e * pn.comps + g) * residual[g]
                row = e * width + k
                coupled[row * n_ch : (row + 1) * n_ch, :] = total
        for row in range(rows):
            iterate[row * n_ch : (row + 1) * n_ch, :] = line(coupled, row)

    loads[4].wait()

    per = 4 if lines % 4 == 0 else 1

    def low_hot(turn, carry):
        for c in range(per):
            chunk = turn * per + c
            low = remainder(slot_buf[pl.ds(chunk, 1), :], pn.width)
            low = jnp.broadcast_to(low, (pn.width, LANES))
            where = pl.ds(pl.multiple_of(chunk * LANES, LANES), LANES)
            right_buf[:, where] = jnp.where(low == iota(low.shape, 0), 1.0, 0.0).astype(BF16)
        return carry

    lax.fori_loop(0, lines // per, low_hot, 0)

    for offset in range(1, pn.rep):
        rep_copy(offset).wait()

    per = 8 if lines % 8 == 0 else 1
    half_dom = pn.dom // 2
    n_slot = half_dom * pn.slot_rows
    slot_half = slice(0, n_slot), slice(n_slot, 2 * n_slot)

    def pack(first_place, turn, carry):
        for c in range(per):
            chunk = turn * per + c
            lanes = slice(c * LANES, (c + 1) * LANES)
            slot = slot_buf[pl.ds(chunk, 1), :]
            owner = chunk // pn.blocks
            column = pl.multiple_of(chunk % pn.blocks * LANES, LANES)
            value = face_buf[owner, :, pl.ds(column, LANES)]
            cell = cell_ref[pl.ds(chunk, 1), :].astype(F32)
            high = jnp.broadcast_to(quotient(slot, pn.width), (8, LANES))
            sub = iota((8, LANES), 0)
            parts = []
            for tile in range(pn.slot_rows // 8):
                row = jnp.zeros((8, LANES), F32)
                for v in range(pn.values + 1):
                    source = value[v : v + 1] if v < pn.values else cell
                    low_row, top_row = v * pn.steps - tile * 8, (v + 1) * pn.steps - tile * 8
                    if top_row <= 0 or low_row >= 8:
                        continue
                    inside = (sub >= low_row) & (sub < top_row)
                    row = jnp.where(inside, jnp.broadcast_to(source, (8, LANES)), row)
                parts.append([part.astype(F32) for part in split(row)])
            halves = ([], [])
            for d in range(half_dom):
                for tile in range(pn.slot_rows // 8):
                    step = remainder(sub + tile * 8, pn.steps)
                    here = high == (first_place + d) * pn.steps + step
                    for half in range(2):
                        halves[half].append(jnp.where(here, parts[tile][half], 0.0))
            for half in range(2):
                left_buf[slot_half[half], lanes] = jnp.concatenate(halves[half], axis=0).astype(BF16)
        where = pl.ds(pl.multiple_of(turn * per * LANES, per * LANES), per * LANES)
        found = dot_last(left_buf[...], right_buf[:, where])
        slot_sum[...] += found[:n_slot] + found[n_slot:]
        return carry

    def dom_copy(place):
        target = lax.rem(me_dom + place + ahead, pn.dom)
        return pltpu.make_async_remote_copy(
            src_ref=pack_buf.at[place],
            dst_ref=recv_buf.at[place],
            send_sem=dom_send_sem.at[place],
            recv_sem=dom_recv_sem.at[place],
            device_id=(target, me_rep),
            device_id_type=MESH,
        )

    def send_faces(place, carry):
        dom_copy(place).start()
        return carry

    own_place = pn.dom - ahead
    filled = pn.values * pn.steps
    for first_place in (0, half_dom):
        slot_sum[...] = jnp.zeros(slot_sum.shape, F32)
        lax.fori_loop(0, lines // per, functools.partial(pack, first_place), 0)
        for d in range(half_dom):
            a = d * pn.slot_rows
            if pn.compact:
                found = slot_sum[a : a + pn.slot_rows, :LANES]
                other = slot_sum[a : a + pn.slot_rows, LANES:]
                pack_buf[first_place + d] = jnp.concatenate(
                    [found[: filled + pn.steps], other[filled : filled + pn.steps], other[:filled]], axis=0
                )
            else:
                for part in range(pn.width // LANES):
                    pack_buf[
                        first_place + d, part * pn.slot_rows : (part + 1) * pn.slot_rows, :
                    ] = slot_sum[a : a + pn.slot_rows, part * LANES : (part + 1) * LANES]
        if first_place == 0:
            lax.fori_loop(0, half_dom, send_faces, 0)
        else:
            lax.fori_loop(half_dom, own_place, send_faces, 0)
            lax.fori_loop(own_place + 1, pn.dom, send_faces, 0)
    recv_buf[own_place] = pack_buf[own_place]

    loads[5].wait()

    def unfold_previous(e, carry):
        for r in range(2):
            unfold(prev_ref[e, r], iterate, (e * width + r * pn.pairs) * n_ch)
        return carry

    lax.fori_loop(0, pn.comps, unfold_previous, 0)
    loads[6].wait()
    field[...] = jnp.zeros(field.shape, F32)
    spread_field()
    one_hot(remainder(send_index(), wide), hot_send)
    send_halo(0)

    for load in loads[7:]:
        load.wait()
    def unfold_jac(index, carry):
        unfold(jac_ref[index].astype(F32), jac, index * (n_faces * n_ch))
        return carry

    lax.fori_loop(0, pn.comps * pn.comps, unfold_jac, 0)
    for face in range(n_faces):
        index = jnp.broadcast_to(neighbor_ref[face : face + 1, :], (8, pn.cells))
        high_buf[face] = quotient(index, wide)
        one_hot(remainder(index, wide), hot_near.at[face])

    def unfold_others(e, carry):
        unfold(diag_ref[e], diag, e * pn.comps * n_ch)
        unfold(weight_ref[e], weight, e * 2 * n_ch)
        for r in range(2):
            unfold(flow_ref[e, r], flow, (e * width + r * pn.pairs) * n_ch)
        return carry

    lax.fori_loop(0, pn.comps, unfold_others, 0)
    take_ghost(0)
    gather_all()
    couple()

    wall_buf[...] = jnp.zeros(wall_buf.shape, F32)
    half_rows = pn.values * n_ch

    def add_faces(offset):
        for step in range(pn.steps):
            for part in range(pn.width // LANES):
                place = step * pn.width + part * LANES
                where = slice(place, place + LANES)
                if pn.compact:
                    top, cell_row = part * pn.slot_rows, filled + step + part * pn.steps
                else:
                    top, cell_row = part * pn.slot_rows, filled + step + part * pn.slot_rows
                cell = recv_buf[offset, cell_row : cell_row + 1, :].astype(jnp.int32)
                low = jnp.broadcast_to(remainder(cell, LANES), (LANES, LANES))
                add_right[:, where] = jnp.where(
                    low == iota((LANES, LANES), 0), 1.0, 0.0
                ).astype(BF16)
                here = jnp.broadcast_to(quotient(cell, LANES), (n_ch, LANES)) == iota((n_ch, LANES), 0)
                for v in range(pn.values):
                    row = top + v * pn.steps + step
                    value = jnp.broadcast_to(recv_buf[offset, row : row + 1, :], (n_ch, LANES))
                    first, second = split(jnp.where(here, value, 0.0))
                    add_left[v * n_ch : (v + 1) * n_ch, where] = first
                    add_left[half_rows + v * n_ch : half_rows + (v + 1) * n_ch, where] = second
        found = dot_last(add_left[...], add_right[...])
        wall_buf[...] += found[:half_rows] + found[half_rows:]

    def receive(offset, carry):
        @pl.when(offset != own_place)
        def arrived():
            dom_copy(offset).wait()

        add_faces(offset)
        return carry

    lax.fori_loop(0, pn.dom, receive, 0)

    def add_wall(e, carry):
        first, second = line(weight, 2 * e), line(weight, 2 * e + 1)
        for k in range(width):
            row = e * width + k
            flow[pl.ds(pl.multiple_of(row * n_ch, n_ch), n_ch), :] = (
                line(flow, row) + first * line(wall_buf, k) + second * line(wall_buf, width + k)
            )
        return carry

    lax.fori_loop(0, pn.comps, add_wall, 0)

    update()
    for sweep in range(1, SWEEPS):
        spread_field()
        send_halo(sweep)
        gather_local()
        take_ghost(sweep)
        gather_ghost()
        couple()
        update()

    def fold_output(e, carry):
        for r in range(2):
            for tile in range(n_ch):
                start = (e * width + r * pn.pairs) * n_ch + tile
                out_ref[e, r, :, tile * LANES : (tile + 1) * LANES] = iterate[
                    pl.ds(start, pn.pairs, stride=n_ch), :
                ]
        return carry

    lax.fori_loop(0, pn.comps, fold_output, 0)


def shards(
    dom,
    rep,
    spline_blocks,
    modal_coeff,
    frequency,
    face_dest,
    face_cell,
    wall_weight,
    flow_rhs,
    previous,
    diag_inverse,
    off_jacobian,
    neighbor,
    send_list,
):
    pn = Plan(dom, rep, spline_blocks, face_dest, flow_rhs, send_list)
    modes = modal_coeff.shape[0]
    operands = (
        frequency,
        jnp.transpose(modal_coeff, (1, 2, 0)).reshape(2 * rep * pn.pairs, modes),
        spline_blocks.reshape(pn.blocks, 2 * modes, LANES),
        face_dest.reshape(pn.face_chunks, LANES),
        face_cell.reshape(pn.face_chunks, LANES),
        previous,
        send_list,
        neighbor,
        jnp.transpose(off_jacobian, (1, 2, 0, 3)).reshape(
            pn.comps * pn.comps, neighbor.shape[0], pn.cells
        ),
        diag_inverse,
        wall_weight,
        flow_rhs,
    )
    n_faces = neighbor.shape[0]
    lines = pn.face_chunks
    per = 8 if pn.face_chunks % 8 == 0 else 1
    vmem = pl.BlockSpec(memory_space=pltpu.VMEM)
    return pl.pallas_call(
        functools.partial(kernel, pn),
        out_shape=jax.ShapeDtypeStruct(previous.shape, F32),
        in_specs=[pl.BlockSpec(memory_space=pltpu.HBM)] * len(operands),
        out_specs=vmem,
        scratch_shapes=[pltpu.SMEM(frequency.shape, F32)]
        + [pltpu.VMEM(value.shape, value.dtype) for value in operands[1:]]
        + [
            pltpu.SemaphoreType.DMA((len(operands),)),
            pltpu.VMEM((rep, pn.values, pn.own_faces), F32),
            pltpu.VMEM((rep, pn.values, pn.own_faces), F32),
            pltpu.VMEM((lines, LANES), jnp.int32),
            pltpu.VMEM((dom * pn.slot_rows, per * LANES), BF16),
            pltpu.VMEM((pn.width, pn.faces), BF16),
            pltpu.VMEM((dom // 2 * pn.slot_rows, pn.width), F32),
            pltpu.VMEM((dom, pn.sent_rows, LANES), F32),
            pltpu.VMEM((dom, pn.sent_rows, LANES), F32),
            pltpu.VMEM((2 * pn.values * pn.chunks, pn.cap), BF16),
            pltpu.VMEM((LANES, pn.cap), BF16),
            pltpu.VMEM((pn.values * pn.chunks, LANES), F32),
            pltpu.VMEM((pn.chunks * pn.row_pad, LANES), F32),
            pltpu.VMEM(((pn.cells + 4 * pn.halo) // pn.wide * pn.rows, 2 * pn.wide), BF16),
            pltpu.VMEM((pn.wide, 4 * pn.halo), BF16),
            pltpu.VMEM((n_faces, pn.wide, pn.cells), BF16),
            pltpu.VMEM((n_faces, 8, pn.cells), jnp.int32),
            pltpu.VMEM((n_faces, pn.row_pad, pn.cells), F32),
            pltpu.VMEM((SWEEPS, 4, pn.row_pad, pn.halo), F32),
            pltpu.VMEM((SWEEPS, 4, pn.row_pad, pn.halo), F32),
            pltpu.VMEM((n_faces * pn.rows * pn.chunks, LANES), F32),
            pltpu.VMEM((n_faces * pn.comps * pn.comps * pn.chunks, LANES), F32),
            pltpu.VMEM((pn.comps * pn.comps * pn.chunks, LANES), F32),
            pltpu.VMEM((pn.comps * 2 * pn.chunks, LANES), F32),
            pltpu.VMEM((pn.rows * pn.chunks, LANES), F32),
            pltpu.VMEM((pn.rows * pn.chunks, LANES), F32),
            pltpu.VMEM((pn.rows * pn.chunks, LANES), F32),
            pltpu.SemaphoreType.DMA((rep,)),
            pltpu.SemaphoreType.DMA((rep,)),
            pltpu.SemaphoreType.DMA((dom,)),
            pltpu.SemaphoreType.DMA((dom,)),
            pltpu.SemaphoreType.DMA((SWEEPS, 4)),
            pltpu.SemaphoreType.DMA((SWEEPS, 4)),
        ],
        compiler_params=pltpu.CompilerParams(
            collective_id=0, has_side_effects=True, vmem_limit_bytes=63 * 1024 * 1024
        ),
    )(*operands)


def solution(mesh):
    return jax.shard_map(
        functools.partial(shards, mesh.shape["dom"], mesh.shape["rep"]),
        mesh=mesh,
        in_specs=(
            P(("dom", "rep"), None, None, None),
            P(),
            P(),
            P("dom", None),
            P("dom"),
            P(None, None, "dom"),
            P(None, None, "rep", "dom"),
            P(None, None, "rep", "dom"),
            P(None, None, "dom"),
            P(None, None, None, "dom"),
            P(None, "dom"),
            P(None, "dom"),
        ),
        out_specs=P(None, None, "rep", "dom"),
        check_vma=False,
    )
```

```python
import functools

import jax
import jax.numpy as jnp
from jax import lax
from jax.experimental import pallas as pl
from jax.experimental.pallas import tpu as pltpu
from jax.sharding import PartitionSpec as P

SWEEPS = 2
OFFSETS = (1, -1, 2, -2)
LANES = 128
MESH = pl.DeviceIdType.MESH
F32 = jnp.float32
BF16 = jnp.bfloat16


def iota(shape, axis):
    return lax.broadcasted_iota(jnp.int32, shape, axis)


def remainder(value, size):
    return value & (size - 1) if size & (size - 1) == 0 else value % size


def quotient(value, size):
    return value >> (size.bit_length() - 1) if size & (size - 1) == 0 else value // size


def split(value):
    high = value.astype(BF16)
    return high, (value - high.astype(F32)).astype(BF16)


def dot_last(a, b):
    return lax.dot_general(a, b, (((1,), (1,)), ((), ())), preferred_element_type=F32)


class Plan:
    def __init__(self, dom, rep, spline, face_dest, flow_rhs, send_list):
        self.dom, self.rep = dom, rep
        self.blocks = spline.shape[0]
        self.faces = face_dest.shape[0]
        self.own_faces = self.faces // rep
        self.pairs = flow_rhs.shape[2]
        self.comps = flow_rhs.shape[0]
        self.cells = flow_rhs.shape[3]
        self.halo = send_list.shape[1]
        self.part_rows = 2 * self.pairs
        self.rows = self.comps * self.part_rows
        self.row_pad = -(-self.rows // 8) * 8
        self.values = 2 * self.part_rows
        self.cap = 2 * self.faces // dom
        self.width = min(2 * LANES, self.cap)
        self.steps = self.cap // self.width
        count = self.values + 1
        while count * self.steps % 8:
            count += 1
        self.slot_rows = count * self.steps
        spare = self.slot_rows - (self.values + 1) * self.steps
        self.compact = self.width == 2 * LANES and spare == self.steps
        self.sent_rows = self.slot_rows * (self.width // LANES)
        if self.compact:
            self.sent_rows -= 2 * self.steps
        self.chunks = self.cells // LANES
        self.wide = min(2 * LANES, self.halo)
        self.face_chunks = self.faces // LANES


def kernel(
    pn,
    *refs,
):
    hbm, out_ref, staged, (load_sem, *refs) = refs[:12], refs[12], refs[13:25], refs[25:]
    (
        freq_ref,
        coeff_ref,
        spline_ref,
        dest_ref,
        cell_ref,
        prev_ref,
        send_ref,
        neighbor_ref,
        jac_ref,
        diag_ref,
        weight_ref,
        flow_ref,
    ) = staged
    (
        part_buf,
        face_buf,
        slot_buf,
        left_buf,
        right_buf,
        slot_sum,
        pack_buf,
        recv_buf,
        add_left,
        add_right,
        wall_buf,
        field,
        table,
        hot_send,
        hot_near,
        high_buf,
        near,
        ghost,
        halo_send,
        beside,
        jac,
        diag,
        weight,
        flow,
        iterate,
        coupled,
        rep_send_sem,
        rep_recv_sem,
        dom_send_sem,
        dom_recv_sem,
        halo_send_sem,
        halo_recv_sem,
    ) = refs
    loads = [pltpu.make_async_copy(hbm[i], staged[i], load_sem.at[i]) for i in range(12)]
    for load in loads:
        load.start()
    me_dom, me_rep = lax.axis_index("dom"), lax.axis_index("rep")
    n_ch, rows, rpad, width = pn.chunks, pn.rows, pn.row_pad, pn.part_rows
    groups = rpad // 8

    barrier = pltpu.get_barrier_semaphore()
    for offset in range(1, pn.rep):
        pl.semaphore_signal(
            barrier, inc=1, device_id=(me_dom, lax.rem(me_rep + offset, pn.rep)), device_id_type=MESH
        )

    def greet(offset, carry):
        pl.semaphore_signal(
            barrier, inc=1, device_id=(lax.rem(me_dom + offset, pn.dom), me_rep), device_id_type=MESH
        )
        return carry

    lax.fori_loop(1, pn.dom, greet, 0)

    row_id = iota((pn.rep * pn.values, LANES), 0)
    pair_id = row_id // pn.values * pn.pairs + row_id % pn.pairs
    scale = jnp.zeros(row_id.shape, F32)
    loads[0].wait()
    for pair in range(pn.rep * pn.pairs):
        scale = jnp.where(pair_id == pair, freq_ref[pair], scale)
    scale = jnp.where(row_id // pn.pairs % 2 == 0, -scale, scale)
    scale = jnp.where(row_id // width % 2 == 0, scale, 1.0)
    loads[1].wait()
    all_pairs = pn.rep * pn.pairs
    shape = (pn.rep * pn.values, 2 * all_pairs)
    row_id, column = iota(shape, 0), iota(shape, 1)
    part_id = row_id // pn.pairs % 2
    pair_id = row_id // pn.values * pn.pairs + row_id % pn.pairs
    coeffs = []
    for q in range(2):
        source = part_id if q == 1 else 1 - part_id
        chosen = (row_id // width % 2 == q) & (column == source * all_pairs + pair_id)
        chosen = jnp.where(chosen, 1.0, 0.0).astype(BF16)
        coeffs.append(jnp.dot(chosen, coeff_ref[...], preferred_element_type=F32).astype(BF16))
    modes = coeff_ref.shape[1]
    loads[2].wait()
    for block in range(pn.blocks):
        base = jnp.dot(coeffs[0], spline_ref[block, :modes], preferred_element_type=F32)
        base += jnp.dot(coeffs[1], spline_ref[block, modes:], preferred_element_type=F32)
        base *= scale
        for peer in range(pn.rep):
            part_buf[peer, :, block * LANES : (block + 1) * LANES] = base[
                peer * pn.values : (peer + 1) * pn.values
            ]

    pl.semaphore_wait(barrier, pn.rep - 1 + pn.dom - 1)

    def rep_copy(offset):
        peer = lax.rem(me_rep + offset, pn.rep)
        return pltpu.make_async_remote_copy(
            src_ref=part_buf.at[peer],
            dst_ref=face_buf.at[me_rep],
            send_sem=rep_send_sem.at[offset],
            recv_sem=rep_recv_sem.at[offset],
            device_id=(me_dom, peer),
            device_id_type=MESH,
        )

    for offset in range(1, pn.rep):
        rep_copy(offset).start()
    face_buf[me_rep] = part_buf[me_rep]

    group = min(8, pn.dom)
    lines = pn.face_chunks
    tri = jnp.where(
        (iota((LANES, 2 * LANES), 1) >= LANES)
        | (iota((LANES, 2 * LANES), 0) <= iota((LANES, 2 * LANES), 1)),
        1.0,
        0.0,
    ).astype(BF16)
    size = group * lines
    above = jnp.where(
        (iota((size, size), 0) // lines == iota((size, size), 1) // lines)
        & (iota((size, size), 1) < iota((size, size), 0)),
        1.0,
        0.0,
    ).astype(BF16)
    loads[3].wait()
    ahead = pn.dom // 4
    dest = remainder(dest_ref[...] - me_dom + (2 * pn.dom - ahead), pn.dom)
    slots = jnp.zeros((lines, LANES), F32)
    for first in range(0, pn.dom, group):
        mask = jnp.concatenate(
            [jnp.where(dest == first + d, 1.0, 0.0) for d in range(group)], axis=0
        )
        counts = jnp.dot(mask.astype(BF16), tri, preferred_element_type=F32)
        before = jnp.dot(above, counts[:, LANES:].astype(BF16), preferred_element_type=F32)
        place = mask * (counts[:, :LANES] + before - 1.0)
        for d in range(group):
            part = slice(d * lines, (d + 1) * lines)
            slots = slots + place[part] + mask[part] * float((first + d) * pn.cap)
    slot_buf[...] = slots.astype(jnp.int32)

    def unfold(source, target, base):
        for tile in range(n_ch):
            target[pl.ds(base + tile, source.shape[0], stride=n_ch), :] = source[
                :, tile * LANES : (tile + 1) * LANES
            ]

    wide, n_wide = pn.wide, pn.cells // pn.wide
    per_wide = wide // LANES
    n_faces = neighbor_ref.shape[0]

    n_full = rows // 8
    sub = iota((8, wide), 0)

    def spread_field():
        for row in range(rows):
            value = iterate[row * n_ch : (row + 1) * n_ch]
            field[pl.ds(row, n_ch, stride=rpad), :] = value
            if row >= n_full * 8:
                field[pl.ds(row + 4, n_ch, stride=rpad), :] = value
        blocks = [
            jnp.concatenate(
                [
                    field[chunk * rpad : (chunk + 1) * rpad, :]
                    for chunk in range(c * per_wide, (c + 1) * per_wide)
                ],
                axis=1,
            )
            for c in range(n_wide)
        ]
        fill_table(blocks, 0)

    def fill_table(blocks, first):
        count = len(blocks)
        tiles = [block[g * 8 : g * 8 + 8] for g in range(n_full) for block in blocks]
        for c in range(count // 2):
            a, b = blocks[c][n_full * 8 :], blocks[c + count // 2][n_full * 8 :]
            tiles.append(jnp.where(sub < 4, a, b))
        where = slice(first, first + len(tiles) * 8)
        table[where, :wide], table[where, wide:] = split(jnp.concatenate(tiles, axis=0))

    def table_rows(count):
        return (n_full * count + count // 2) * 8

    near_rows, far_rows = table_rows(n_wide), table_rows(4 * pn.halo // wide)

    def multiply(first, count, hot):
        return jnp.dot(
            table[first : first + count, :],
            jnp.concatenate([hot, hot], axis=0),
            preferred_element_type=F32,
        )

    def choose(found, first_chunk, count, high, start):
        picked = list(start)
        late = jnp.where(iota(high.shape, 0) < 4, high, high - count // 2)
        for chunk in range(count):
            here = high == first_chunk + chunk
            for g in range(n_full):
                at = (g * count + chunk) * 8
                picked[g] = jnp.where(here, found[at : at + 8], picked[g])
        for chunk in range(count // 2):
            at = (n_full * count + chunk) * 8
            picked[n_full] = jnp.where(
                late == first_chunk + chunk, found[at : at + 8], picked[n_full]
            )
        return picked

    def joined(picked):
        return picked[:n_full] + [picked[n_full] + pltpu.roll(picked[n_full], 4, axis=0)]

    def one_hot(low, target):
        both = jnp.concatenate([low, low], axis=0)

        def body(turn, carry):
            for part in range(4):
                first = pl.multiple_of(turn * 64 + part * 16, 16)
                target[pl.ds(first, 16), :] = jnp.where(
                    both == iota(both.shape, 0) + first, 1.0, 0.0
                ).astype(BF16)
            return carry

        lax.fori_loop(0, wide // 64, body, 0)

    def halo_copy(sweep, block):
        return pltpu.make_async_remote_copy(
            src_ref=halo_send.at[sweep, block],
            dst_ref=ghost.at[sweep, block],
            send_sem=halo_send_sem.at[sweep, block],
            recv_sem=halo_recv_sem.at[sweep, block],
            device_id=(lax.rem(me_dom + OFFSETS[block] + pn.dom, pn.dom), me_rep),
            device_id_type=MESH,
        )

    def send_index():
        return jnp.concatenate(
            [jnp.broadcast_to(send_ref[k : k + 1, :], (8, pn.halo)) for k in range(4)], axis=1
        )

    def send_halo(sweep):
        high = quotient(send_index(), wide)
        zeros = [jnp.zeros(high.shape, F32)] * groups
        found = joined(choose(multiply(0, near_rows, hot_send[...]), 0, n_wide, high, zeros))
        for block in range(4):
            for g in range(groups):
                halo_send[sweep, block, g * 8 : g * 8 + 8, :] = found[g][
                    :, block * pn.halo : (block + 1) * pn.halo
                ]
            halo_copy(sweep, block).start()

    n_ghost = pn.halo // wide

    def take_ghost(sweep):
        for block in range(4):
            halo_copy(sweep, block).wait()
        blocks = []
        for chunk in range(4 * n_ghost):
            lane = chunk % n_ghost * wide
            blocks.append(ghost[sweep, chunk // n_ghost, :, lane : lane + wide])
        fill_table(blocks, near_rows)

    def keep_beside(face, picked):
        found = joined(picked)
        for g in range(groups):
            count = min(8, rows - g * 8)
            for tile in range(n_ch):
                where = pl.ds((face * rows + g * 8) * n_ch + tile, count, stride=n_ch)
                beside[where, :] = found[g][:count, tile * LANES : (tile + 1) * LANES]

    def gather_local():
        def body(face, carry):
            high = high_buf[face]
            zeros = [jnp.zeros(high.shape, F32)] * groups
            found = choose(multiply(0, near_rows, hot_near[face]), 0, n_wide, high, zeros)
            for g in range(groups):
                near[face, g * 8 : g * 8 + 8, :] = found[g]
            return carry

        lax.fori_loop(0, n_faces, body, 0)

    def gather_ghost():
        def body(face, carry):
            start = [near[face, g * 8 : g * 8 + 8, :] for g in range(groups)]
            found = multiply(near_rows, far_rows, hot_near[face])
            keep_beside(face, choose(found, n_wide, 4 * n_ghost, high_buf[face], start))
            return carry

        lax.fori_loop(0, n_faces, body, 0)

    def line(ref, index):
        return ref[pl.ds(pl.multiple_of(index * n_ch, n_ch), n_ch), :]

    def couple():
        def body(e, carry):
            total = [jnp.zeros((n_ch, LANES), F32)] * width
            for face in range(n_faces):
                for g in range(pn.comps):
                    entry = line(jac, (e * pn.comps + g) * n_faces + face)
                    for k in range(width):
                        total[k] = total[k] + entry * line(beside, face * rows + g * width + k)
            for k in range(width):
                coupled[pl.ds(pl.multiple_of((e * width + k) * n_ch, n_ch), n_ch), :] = total[k]
            return carry

        lax.fori_loop(0, pn.comps, body, 0)

    def update():
        own = [freq_ref[me_rep * pn.pairs + p] for p in range(pn.pairs)]
        for k in range(width):
            part, pair = k // pn.pairs, k % pn.pairs
            turned = (1 - part) * pn.pairs + pair
            sign = own[pair] if part == 0 else -own[pair]
            residual = []
            for g in range(pn.comps):
                row = g * width + k
                residual.append(
                    line(flow, row) - line(coupled, row) + sign * line(iterate, g * width + turned)
                )
            for e in range(pn.comps):
                total = line(diag, e * pn.comps) * residual[0]
                for g in range(1, pn.comps):
                    total = total + line(diag, e * pn.comps + g) * residual[g]
                row = e * width + k
                coupled[row * n_ch : (row + 1) * n_ch, :] = total
        for row in range(rows):
            iterate[row * n_ch : (row + 1) * n_ch, :] = line(coupled, row)

    loads[4].wait()

    per = 4 if lines % 4 == 0 else 1

    def low_hot(turn, carry):
        for c in range(per):
            chunk = turn * per + c
            low = remainder(slot_buf[pl.ds(chunk, 1), :], pn.width)
            low = jnp.broadcast_to(low, (pn.width, LANES))
            where = pl.ds(pl.multiple_of(chunk * LANES, LANES), LANES)
            right_buf[:, where] = jnp.where(low == iota(low.shape, 0), 1.0, 0.0).astype(BF16)
        return carry

    lax.fori_loop(0, lines // per, low_hot, 0)

    for offset in range(1, pn.rep):
        rep_copy(offset).wait()

    per = 8 if lines % 8 == 0 else 1
    half_dom = pn.dom // 2
    n_slot = half_dom * pn.slot_rows
    slot_half = slice(0, n_slot), slice(n_slot, 2 * n_slot)

    def pack(first_place, turn, carry):
        for c in range(per):
            chunk = turn * per + c
            lanes = slice(c * LANES, (c + 1) * LANES)
            slot = slot_buf[pl.ds(chunk, 1), :]
            owner = chunk // pn.blocks
            column = pl.multiple_of(chunk % pn.blocks * LANES, LANES)
            value = face_buf[owner, :, pl.ds(column, LANES)]
            cell = cell_ref[pl.ds(chunk, 1), :].astype(F32)
            high = jnp.broadcast_to(quotient(slot, pn.width), (8, LANES))
            sub = iota((8, LANES), 0)
            parts = []
            for tile in range(pn.slot_rows // 8):
                row = jnp.zeros((8, LANES), F32)
                for v in range(pn.values + 1):
                    source = value[v : v + 1] if v < pn.values else cell
                    low_row, top_row = v * pn.steps - tile * 8, (v + 1) * pn.steps - tile * 8
                    if top_row <= 0 or low_row >= 8:
                        continue
                    inside = (sub >= low_row) & (sub < top_row)
                    row = jnp.where(inside, jnp.broadcast_to(source, (8, LANES)), row)
                parts.append([part.astype(F32) for part in split(row)])
            halves = ([], [])
            for d in range(half_dom):
                for tile in range(pn.slot_rows // 8):
                    step = remainder(sub + tile * 8, pn.steps)
                    here = high == (first_place + d) * pn.steps + step
                    for half in range(2):
                        halves[half].append(jnp.where(here, parts[tile][half], 0.0))
            for half in range(2):
                left_buf[slot_half[half], lanes] = jnp.concatenate(halves[half], axis=0).astype(BF16)
        where = pl.ds(pl.multiple_of(turn * per * LANES, per * LANES), per * LANES)
        found = dot_last(left_buf[...], right_buf[:, where])
        slot_sum[...] += found[:n_slot] + found[n_slot:]
        return carry

    def dom_copy(place):
        target = lax.rem(me_dom + place + ahead, pn.dom)
        return pltpu.make_async_remote_copy(
            src_ref=pack_buf.at[place],
            dst_ref=recv_buf.at[place],
            send_sem=dom_send_sem.at[place],
            recv_sem=dom_recv_sem.at[place],
            device_id=(target, me_rep),
            device_id_type=MESH,
        )

    def send_faces(place, carry):
        dom_copy(place).start()
        return carry

    def start_sweeps():
        loads[5].wait()

        def unfold_previous(e, carry):
            for r in range(2):
                unfold(prev_ref[e, r], iterate, (e * width + r * pn.pairs) * n_ch)
            return carry

        lax.fori_loop(0, pn.comps, unfold_previous, 0)
        loads[6].wait()
        field[...] = jnp.zeros(field.shape, F32)
        spread_field()
        one_hot(remainder(send_index(), wide), hot_send)
        send_halo(0)

    own_place = pn.dom - ahead
    filled = pn.values * pn.steps
    for first_place in (0, half_dom):
        slot_sum[...] = jnp.zeros(slot_sum.shape, F32)
        lax.fori_loop(0, lines // per, functools.partial(pack, first_place), 0)
        for d in range(half_dom):
            a = d * pn.slot_rows
            if pn.compact:
                found = slot_sum[a : a + pn.slot_rows, :LANES]
                other = slot_sum[a : a + pn.slot_rows, LANES:]
                pack_buf[first_place + d] = jnp.concatenate(
                    [found[: filled + pn.steps], other[filled : filled + pn.steps], other[:filled]], axis=0
                )
            else:
                for part in range(pn.width // LANES):
                    pack_buf[
                        first_place + d, part * pn.slot_rows : (part + 1) * pn.slot_rows, :
                    ] = slot_sum[a : a + pn.slot_rows, part * LANES : (part + 1) * LANES]
        if first_place == 0:
            lax.fori_loop(0, half_dom, send_faces, 0)
            start_sweeps()
        else:
            lax.fori_loop(half_dom, own_place, send_faces, 0)
            lax.fori_loop(own_place + 1, pn.dom, send_faces, 0)
    recv_buf[own_place] = pack_buf[own_place]

    for load in loads[7:]:
        load.wait()
    def unfold_jac(index, carry):
        unfold(jac_ref[index].astype(F32), jac, index * (n_faces * n_ch))
        return carry

    lax.fori_loop(0, pn.comps * pn.comps, unfold_jac, 0)
    for face in range(n_faces):
        index = jnp.broadcast_to(neighbor_ref[face : face + 1, :], (8, pn.cells))
        high_buf[face] = quotient(index, wide)
        one_hot(remainder(index, wide), hot_near.at[face])

    def unfold_others(e, carry):
        unfold(diag_ref[e], diag, e * pn.comps * n_ch)
        unfold(weight_ref[e], weight, e * 2 * n_ch)
        for r in range(2):
            unfold(flow_ref[e, r], flow, (e * width + r * pn.pairs) * n_ch)
        return carry

    lax.fori_loop(0, pn.comps, unfold_others, 0)
    gather_local()
    take_ghost(0)
    gather_ghost()
    couple()

    wall_buf[...] = jnp.zeros(wall_buf.shape, F32)
    half_rows = pn.values * n_ch

    def add_faces(offset):
        for step in range(pn.steps):
            for part in range(pn.width // LANES):
                place = step * pn.width + part * LANES
                where = slice(place, place + LANES)
                if pn.compact:
                    top, cell_row = part * pn.slot_rows, filled + step + part * pn.steps
                else:
                    top, cell_row = part * pn.slot_rows, filled + step + part * pn.slot_rows
                cell = recv_buf[offset, cell_row : cell_row + 1, :].astype(jnp.int32)
                low = jnp.broadcast_to(remainder(cell, LANES), (LANES, LANES))
                add_right[:, where] = jnp.where(
                    low == iota((LANES, LANES), 0), 1.0, 0.0
                ).astype(BF16)
                here = jnp.broadcast_to(quotient(cell, LANES), (n_ch, LANES)) == iota((n_ch, LANES), 0)
                for v in range(pn.values):
                    row = top + v * pn.steps + step
                    value = jnp.broadcast_to(recv_buf[offset, row : row + 1, :], (n_ch, LANES))
                    first, second = split(jnp.where(here, value, 0.0))
                    add_left[v * n_ch : (v + 1) * n_ch, where] = first
                    add_left[half_rows + v * n_ch : half_rows + (v + 1) * n_ch, where] = second
        found = dot_last(add_left[...], add_right[...])
        wall_buf[...] += found[:half_rows] + found[half_rows:]

    def receive(offset, carry):
        @pl.when(offset != own_place)
        def arrived():
            dom_copy(offset).wait()

        add_faces(offset)
        return carry

    lax.fori_loop(0, pn.dom, receive, 0)

    def add_wall(e, carry):
        first, second = line(weight, 2 * e), line(weight, 2 * e + 1)
        for k in range(width):
            row = e * width + k
            flow[pl.ds(pl.multiple_of(row * n_ch, n_ch), n_ch), :] = (
                line(flow, row) + first * line(wall_buf, k) + second * line(wall_buf, width + k)
            )
        return carry

    lax.fori_loop(0, pn.comps, add_wall, 0)

    update()
    for sweep in range(1, SWEEPS):
        spread_field()
        send_halo(sweep)
        gather_local()
        take_ghost(sweep)
        gather_ghost()
        couple()
        update()

    def fold_output(e, carry):
        for r in range(2):
            for tile in range(n_ch):
                start = (e * width + r * pn.pairs) * n_ch + tile
                out_ref[e, r, :, tile * LANES : (tile + 1) * LANES] = iterate[
                    pl.ds(start, pn.pairs, stride=n_ch), :
                ]
        return carry

    lax.fori_loop(0, pn.comps, fold_output, 0)


def shards(
    dom,
    rep,
    spline_blocks,
    modal_coeff,
    frequency,
    face_dest,
    face_cell,
    wall_weight,
    flow_rhs,
    previous,
    diag_inverse,
    off_jacobian,
    neighbor,
    send_list,
):
    pn = Plan(dom, rep, spline_blocks, face_dest, flow_rhs, send_list)
    modes = modal_coeff.shape[0]
    operands = (
        frequency,
        jnp.transpose(modal_coeff, (1, 2, 0)).reshape(2 * rep * pn.pairs, modes),
        spline_blocks.reshape(pn.blocks, 2 * modes, LANES),
        face_dest.reshape(pn.face_chunks, LANES),
        face_cell.reshape(pn.face_chunks, LANES),
        previous,
        send_list,
        neighbor,
        jnp.transpose(off_jacobian, (1, 2, 0, 3)).reshape(
            pn.comps * pn.comps, neighbor.shape[0], pn.cells
        ),
        diag_inverse,
        wall_weight,
        flow_rhs,
    )
    n_faces = neighbor.shape[0]
    lines = pn.face_chunks
    per = 8 if pn.face_chunks % 8 == 0 else 1
    vmem = pl.BlockSpec(memory_space=pltpu.VMEM)
    return pl.pallas_call(
        functools.partial(kernel, pn),
        out_shape=jax.ShapeDtypeStruct(previous.shape, F32),
        in_specs=[pl.BlockSpec(memory_space=pltpu.HBM)] * len(operands),
        out_specs=vmem,
        scratch_shapes=[pltpu.SMEM(frequency.shape, F32)]
        + [pltpu.VMEM(value.shape, value.dtype) for value in operands[1:]]
        + [
            pltpu.SemaphoreType.DMA((len(operands),)),
            pltpu.VMEM((rep, pn.values, pn.own_faces), F32),
            pltpu.VMEM((rep, pn.values, pn.own_faces), F32),
            pltpu.VMEM((lines, LANES), jnp.int32),
            pltpu.VMEM((dom * pn.slot_rows, per * LANES), BF16),
            pltpu.VMEM((pn.width, pn.faces), BF16),
            pltpu.VMEM((dom // 2 * pn.slot_rows, pn.width), F32),
            pltpu.VMEM((dom, pn.sent_rows, LANES), F32),
            pltpu.VMEM((dom, pn.sent_rows, LANES), F32),
            pltpu.VMEM((2 * pn.values * pn.chunks, pn.cap), BF16),
            pltpu.VMEM((LANES, pn.cap), BF16),
            pltpu.VMEM((pn.values * pn.chunks, LANES), F32),
            pltpu.VMEM((pn.chunks * pn.row_pad, LANES), F32),
            pltpu.VMEM(((pn.cells + 4 * pn.halo) // pn.wide * pn.rows, 2 * pn.wide), BF16),
            pltpu.VMEM((pn.wide, 4 * pn.halo), BF16),
            pltpu.VMEM((n_faces, pn.wide, pn.cells), BF16),
            pltpu.VMEM((n_faces, 8, pn.cells), jnp.int32),
            pltpu.VMEM((n_faces, pn.row_pad, pn.cells), F32),
            pltpu.VMEM((SWEEPS, 4, pn.row_pad, pn.halo), F32),
            pltpu.VMEM((SWEEPS, 4, pn.row_pad, pn.halo), F32),
            pltpu.VMEM((n_faces * pn.rows * pn.chunks, LANES), F32),
            pltpu.VMEM((n_faces * pn.comps * pn.comps * pn.chunks, LANES), F32),
            pltpu.VMEM((pn.comps * pn.comps * pn.chunks, LANES), F32),
            pltpu.VMEM((pn.comps * 2 * pn.chunks, LANES), F32),
            pltpu.VMEM((pn.rows * pn.chunks, LANES), F32),
            pltpu.VMEM((pn.rows * pn.chunks, LANES), F32),
            pltpu.VMEM((pn.rows * pn.chunks, LANES), F32),
            pltpu.SemaphoreType.DMA((rep,)),
            pltpu.SemaphoreType.DMA((rep,)),
            pltpu.SemaphoreType.DMA((dom,)),
            pltpu.SemaphoreType.DMA((dom,)),
            pltpu.SemaphoreType.DMA((SWEEPS, 4)),
            pltpu.SemaphoreType.DMA((SWEEPS, 4)),
        ],
        compiler_params=pltpu.CompilerParams(
            collective_id=0, has_side_effects=True, vmem_limit_bytes=63 * 1024 * 1024
        ),
    )(*operands)


def solution(mesh):
    return jax.shard_map(
        functools.partial(shards, mesh.shape["dom"], mesh.shape["rep"]),
        mesh=mesh,
        in_specs=(
            P(("dom", "rep"), None, None, None),
            P(),
            P(),
            P("dom", None),
            P("dom"),
            P(None, None, "dom"),
            P(None, None, "rep", "dom"),
            P(None, None, "rep", "dom"),
            P(None, None, "dom"),
            P(None, None, None, "dom"),
            P(None, "dom"),
            P(None, "dom"),
        ),
        out_specs=P(None, None, "rep", "dom"),
        check_vma=False,
    )
```
